128 devices in a mesh: left: 8 (over z, core), right: 16 (over x, y).
Axes of the slice: x: 4, y: 4, z: 4, core: 2. Of those that a mesh axis runs over, the one named last changes fastest.
Arguments:
- psi: bfloat16 [32, 512, 32, 512], P('left', None, 'right'), may hold values from -6 to 6
- env_left: bfloat16 [2, 32, 512, 512], P(None, 'left'), may hold values from -0.25 to 0.25
- env_right: bfloat16 [2, 32, 512, 512], P(None, 'right'), may hold values from -0.25 to 0.25
- left_target: int32 [2, 32], replicated, may hold values from 0 to 31, each once within a row
- right_target: int32 [2, 32], replicated, may hold values from 0 to 31, each once within a row
- qn_left: int32 [32], replicated, may hold values from 0 to 3
- qn_right: int32 [32], replicated, may hold values from 0 to 3
Outputs:
- sigma: bfloat16 [32, 512, 32, 512], P(None, ('left', 'right'))
The draws below stay inside these ranges and needn't reach their ends.
Inputs may be any that keep to these rules, and one draw needn't show every extreme that they name: `left_target`: each row names every left sector exactly once. `right_target`: each row names every right sector exactly once.
All inputs are finite; a program needn't handle non-finite values.
Results may differ from the reference program's by a relative error of at most 0.0058.
Values may be sent and summed in bfloat16 or wider, within the bound.
A program may use at most 128 MiB of HBM per device.

```python
import jax
import jax.numpy as jnp

B = 512
SL = 32
SR = 32
TERMS = 2


def set_ends(drawn, own_key, low, top_value):
    longest = drawn.shape.index(max(drawn.shape))
    spots = []
    for shift in (0, 1):
        where = [jax.random.randint(jax.random.fold_in(own_key, axis), (), 0, length) for axis, length in enumerate(drawn.shape)]
        where[longest] = (where[longest] + shift) % drawn.shape[longest]
        spots.append(tuple(where))
    return drawn.at[spots[0]].set(low).at[spots[1]].set(top_value)


def block_scale(rng, extent, shards, smallest, high):
    loudness, own = 1.0, jax.random.fold_in(rng, 6)
    for position, blocks in shards:
        steps = jnp.exp(jax.random.uniform(jax.random.fold_in(own, position), (blocks,), jnp.float32, smallest / len(shards), high / len(shards)))
        loudness = loudness * jnp.repeat(steps, extent[position] // blocks).reshape([-1 if axis == position else 1 for axis in range(len(extent))])
    return loudness


def normal_values(stream_key, dims, width, most, split=(), dtype=jnp.bfloat16):
    level = block_scale(stream_key, dims, split, -0.22, 0.18) if split else 1.0
    values = jax.random.normal(stream_key, dims, jnp.float32) * width * level
    return jnp.minimum(jnp.maximum(values, -most), most).astype(dtype)


def setup_inputs(seed: int = 0) -> dict:
    arg_keys = jax.random.split(jax.random.key(seed), 8)
    return {
        "psi": normal_values(arg_keys[0], (SL, B, SR, B), 1.0, 6.0, ((0, 8), (2, 16))),
        "env_left": normal_values(arg_keys[1], (TERMS, SL, B, B), B ** -0.5, 0.25, ((1, 8),)),
        "env_right": normal_values(arg_keys[2], (TERMS, SR, B, B), B ** -0.5, 0.25, ((1, 16),)),
        "left_target": jax.vmap(lambda own: jax.random.permutation(own, SL))(jax.random.split(arg_keys[3], TERMS)).reshape((TERMS, SL)).astype(jnp.int32),
        "right_target": jax.vmap(lambda own: jax.random.permutation(own, SR))(jax.random.split(arg_keys[4], TERMS)).reshape((TERMS, SR)).astype(jnp.int32),
        "qn_left": set_ends(jax.random.randint(arg_keys[5], (SL,), 0, 4), jax.random.fold_in(arg_keys[5], 1), 0, 3).astype(jnp.int32),
        "qn_right": set_ends(jax.random.randint(arg_keys[6], (SR,), 0, 4), jax.random.fold_in(arg_keys[6], 1), 0, 3).astype(jnp.int32),
    }


filling_charge = 3


def reference(psi, env_left, env_right, left_target, right_target, qn_left, qn_right):
    total = jnp.zeros(psi.shape, jnp.float32)
    psi_wide = psi.astype(jnp.float32)
    for term in range(TERMS):
        half = jnp.einsum('axy,aybz->axbz', env_left[term].astype(jnp.float32), psi_wide).astype(jnp.bfloat16)
        moved = jnp.einsum('axbz,bwz->axbw', half.astype(jnp.float32), env_right[term].astype(jnp.float32)).astype(jnp.bfloat16)
        inverse_left = jnp.argsort(left_target[term]).astype(jnp.int32)
        inverse_right = jnp.argsort(right_target[term]).astype(jnp.int32)
        placed = jnp.take(jnp.take(moved, inverse_left, axis=0), inverse_right, axis=2)
        total = total + placed.astype(jnp.float32)
    allowed = (qn_left[:, None] + qn_right[None, :]) == filling_charge
    return jnp.where(allowed[:, None, :, None], total, 0.0).astype(jnp.bfloat16)
```

```python
import functools

import jax
import jax.numpy as jnp
from jax import lax
from jax.experimental import pallas as pl
from jax.experimental.pallas import tpu as pltpu
from jax.sharding import Mesh, PartitionSpec as P

filling_charge = 3
B = 512
SECTORS = 32
TERMS = 2
CHIPS_Z = 4
CORES = 2
RIGHT = 16
CHIPS = CHIPS_Z * RIGHT
LEFT_DEV = SECTORS // (CHIPS_Z * CORES)
RIGHT_DEV = SECTORS // RIGHT
ITEMS = TERMS * LEFT_DEV * RIGHT_DEV
HALF = B // CORES
ROWS = B // (CHIPS * CORES)
MESH = pl.DeviceIdType.MESH
VMEM_LIMIT = 60 * 2**20
SIZES = ((12, 12), (12, 14), (12, 16), (16, 20), (16, 32))


def table_kernel(left_target, right_target, qn_left, qn_right, items, sources, labels, most):
    f32, bf16 = jnp.float32, jnp.bfloat16
    square = (SECTORS, SECTORS)
    row = lax.broadcasted_iota(jnp.int32, square, 0)
    column = lax.broadcasted_iota(jnp.int32, square, 1)
    wide = lambda value: value.astype(f32)
    dot = lambda a, b: jnp.dot(a.astype(bf16), b.astype(bf16), preferred_element_type=f32)
    upright = lambda line: jnp.sum(
        jnp.where(row == column, wide(line), 0.0), axis=1, keepdims=True
    )
    charge_left = qn_left[...]
    charge_right = upright(qn_right[...])

    pair = wide(row // RIGHT_DEV == column // RIGHT_DEV)
    second = wide((row + 1 == column) & (column % RIGHT_DEV == 1))
    same = row // LEFT_DEV == column // LEFT_DEV
    core = wide(row // LEFT_DEV % CORES)
    swap = wide(column == row + LEFT_DEV - 2 * LEFT_DEV * (row // LEFT_DEV % CORES))
    active, to_left, to_right, rank, total = [], [], [], [], []
    for t in range(TERMS):
        lefts = upright(left_target[t : t + 1, :])
        rights = wide(right_target[t : t + 1, :])
        hit_left = wide(column) == lefts
        hit_right = wide(row) == rights
        have_left = jnp.sum(jnp.where(hit_left, wide(charge_left), 0.0), axis=1, keepdims=True)
        have_right = jnp.sum(jnp.where(hit_right, charge_right, 0.0), axis=0, keepdims=True)
        allowed = have_left + have_right == float(filling_charge)
        ones = jnp.where(allowed, 1.0, 0.0)
        count = dot(ones, pair)
        active.append(allowed)
        to_left.append(lefts)
        to_right.append(rights)
        rank.append(dot(wide(same & (column < row)), count) + dot(ones, second))
        total.append(dot(wide(same), count))
    rank[1] = rank[1] + total[0]
    own = total[0] + total[1]
    other = dot(swap, own)
    slot = [r + jnp.minimum(other, r + core) for r in rank]

    lane = lax.broadcasted_iota(jnp.int32, (SECTORS, 128), 1)
    tall = lax.broadcasted_iota(jnp.int32, (SECTORS, 128), 0)
    device_lane = tall // RIGHT_DEV == lane % RIGHT
    device_row = tall // LEFT_DEV == lane // RIGHT
    chip_row = tall // (CORES * LEFT_DEV) == lane % CHIPS // RIGHT

    def spread(steps, place, values, rows):
        stack = []
        for k in steps:
            picked = jnp.zeros(square, f32)
            for t in range(TERMS):
                picked = picked + jnp.where(
                    active[t] & (place[t] == float(k)), values[t], 0.0
                )
            stack.append(picked.astype(bf16))
        lanes = dot(jnp.concatenate(stack, axis=0), wide(device_lane))
        lanes = lanes.reshape(len(stack), SECTORS, 128)
        return jnp.sum(jnp.where(rows[None], lanes, 0.0), axis=1)

    item = wide(row % LEFT_DEV * RIGHT_DEV + column % RIGHT_DEV)
    items[...] = spread(
        range(ITEMS), rank, [item, item + float(LEFT_DEV * RIGHT_DEV)], device_row
    ).astype(jnp.int32)

    half_lane = lax.broadcasted_iota(jnp.int32, (ITEMS, 128), 1)

    def by_slot(values):
        both = spread(
            [*range(0, 2 * ITEMS, 2), *range(1, 2 * ITEMS, 2)], slot, values, chip_row
        )
        return jnp.where(half_lane < CHIPS, both[:ITEMS], both[ITEMS:])

    sources[...] = by_slot([core * ITEMS + r for r in rank]).astype(jnp.int32)
    full = jnp.zeros(square, f32)
    high = by_slot([full + lefts + 1.0 for lefts in to_left])
    low = by_slot([full + rights for rights in to_right])
    labels[...] = ((high - 1.0) * SECTORS + low).astype(jnp.int32)
    most_device = jnp.max(own)
    most_chip = jnp.max(own + other)
    choice = jnp.int32(0)
    for depth, slots in SIZES[:-1]:
        choice = choice + jnp.where(
            (most_device > float(depth)) | (most_chip > float(slots)), 1, 0
        )
    most[0, 0] = choice


def tables(left_target, right_target, qn_left, qn_right):
    vmem = pl.BlockSpec(memory_space=pltpu.VMEM)
    table = jax.ShapeDtypeStruct((ITEMS, 128), jnp.int32)
    return pl.pallas_call(
        table_kernel,
        name="tables",
        out_shape=[table, table, table, jax.ShapeDtypeStruct((1, 1), jnp.int32)],
        in_specs=[vmem] * 4,
        out_specs=[vmem] * 3 + [pl.BlockSpec(memory_space=pltpu.SMEM)],
        cost_estimate=pl.CostEstimate(flops=2**24, bytes_accessed=2**15, transcendentals=0),
    )(
        left_target,
        right_target,
        qn_left.reshape(1, SECTORS),
        qn_right.reshape(1, SECTORS),
    )


def last_count(slots):
    return 2 if slots % 4 else 4


def last_shape(count):
    return ROWS * 4 // count, count * CHIPS, B * count // 4


def onehot_rows(label, first, shape):
    row = first + lax.broadcasted_iota(jnp.int32, shape, 0)
    return jnp.where(row == label, 1.0, 0.0).astype(jnp.bfloat16)


def label_of(labels, first, count):
    return jnp.concatenate(
        [labels[pl.ds(first // 2 + p, 1), :] for p in range(count // 2)], axis=1
    )


def exchange_kernel(
    depth,
    slots,
    items,
    sources,
    labels,
    psi_hbm,
    left_hbm,
    right_hbm,
    out,
    last,
    landed,
    psi,
    left,
    right,
    product,
    both,
    send,
    arrived,
    send_pair,
    arrived_pair,
    partial,
    ordered,
    ordered_pair,
    in_sem,
    own_sem,
    pair_send_sem,
    pair_recv_sem,
    free_sem,
    self_sem,
    send_sem,
    recv_sem,
    out_sem,
):
    z = lax.axis_index("z")
    core = lax.axis_index("core")
    place = lax.axis_index("right")
    other = 1 - core
    partner = (z, other, place)
    here = z * RIGHT + place
    device = (z * CORES + core) * RIGHT + place
    fours = slots // 4
    stages = depth // 4
    ends_in_pair = slots % 4 == 2

    psi_rows = psi_hbm.reshape(LEFT_DEV, B * RIGHT_DEV, B)
    psi_load = [
        pltpu.make_async_copy(psi_rows.at[a], landed.at[a], in_sem.at[a])
        for a in range(LEFT_DEV)
    ]
    left_load = pltpu.make_async_copy(left_hbm, left, in_sem.at[LEFT_DEV])
    right_load = pltpu.make_async_copy(right_hbm, right, in_sem.at[LEFT_DEV + 1])
    for load in (*psi_load, left_load, right_load):
        load.start()

    steps = (1, 3, 2, 0)
    route = []
    for i in range(RIGHT):
        step_x = steps[i % 4]
        step_y = steps[(i + i // 4) % 4]
        far_place = (place // 4 + step_x) % 4 * 4 + (place % 4 + step_y) % 4
        route.append((step_x + step_y, steps[(i + i // 4 * 2) % 4], far_place))

    def for_others(visit):
        def turn(shift, carry):
            far_z = [(z + shift + step) % CHIPS_Z for step in range(CHIPS_Z)]
            for moved, step, far_place in route:
                if moved or step:
                    visit(far_z[step], far_place)
                else:
                    pl.when(shift > 0)(functools.partial(visit, far_z[step], far_place))
            return carry

        lax.fori_loop(0, CHIPS_Z, turn, 0)

    barrier = pltpu.get_barrier_semaphore()
    pl.semaphore_signal(barrier, inc=1, device_id=partner, device_id_type=MESH)

    def greet(far_z, far_place):
        pl.semaphore_signal(
            barrier, inc=1, device_id=(far_z, core, far_place), device_id_type=MESH
        )

    for_others(greet)

    def exchange(shape_from, shape_to):
        row = lax.broadcasted_iota(jnp.int32, (256, 256), 0)
        column = lax.broadcasted_iota(jnp.int32, (256, 256), 1)
        source = row % shape_from * shape_to + row // shape_from
        return jnp.where(column == source, 1.0, 0.0).astype(jnp.bfloat16)

    def reorder(onehot, rows):
        return jnp.dot(onehot, rows, preferred_element_type=jnp.float32).astype(
            jnp.bfloat16
        )

    unmix = exchange(128, RIGHT_DEV)

    def split(a, carry):
        pltpu.make_async_copy(psi_rows.at[a], landed.at[a], in_sem.at[a]).wait()
        for part in range(B // 128):
            apart = reorder(unmix, landed[a, part * 256 : part * 256 + 256, :])
            for b in range(RIGHT_DEV):
                psi[a * RIGHT_DEV + b, part * 128 : part * 128 + 128, :] = apart[
                    b * 128 : (b + 1) * 128
                ]
        return carry

    lax.fori_loop(0, LEFT_DEV, split, 0)
    left_load.wait()
    right_load.wait()

    def own_copy(rank):
        return pltpu.make_async_copy(
            product.at[rank, :, core], both.at[core * depth + rank], own_sem.at[rank]
        )

    def pair_copy(rank):
        return pltpu.make_async_remote_copy(
            src_ref=product.at[rank, :, other],
            dst_ref=both.at[core * depth + rank],
            send_sem=pair_send_sem.at[rank],
            recv_sem=pair_recv_sem.at[rank],
            device_id=partner,
            device_id_type=MESH,
        )

    def multiply(rank, carry):
        item = items[rank, device]
        term = item // (LEFT_DEV * RIGHT_DEV)
        pair = item % (LEFT_DEV * RIGHT_DEV)
        half = jnp.dot(
            left[term * LEFT_DEV + pair // RIGHT_DEV],
            psi[pair],
            preferred_element_type=jnp.float32,
        ).astype(jnp.bfloat16)
        moved = lax.dot_general(
            half,
            right[term * RIGHT_DEV + pair % RIGHT_DEV],
            (((1,), (1,)), ((), ())),
            preferred_element_type=jnp.float32,
        ).astype(jnp.bfloat16)
        product[rank] = moved.reshape(CHIPS_Z, CORES, B // (CHIPS_Z * CORES), B)

        @pl.when(rank == 0)
        def _():
            pl.semaphore_wait(barrier, CHIPS)

        @pl.when((rank > 0) & (rank % 4 == 0))
        def _():
            pl.semaphore_wait(free_sem, 1)

        pair_copy(rank).start()
        own_copy(rank).start()
        return carry

    def arrive(rank, carry):
        own_copy(rank).wait()
        pair_copy(rank).wait_recv()
        return carry

    def departing(outgoing, incoming, chunk, far_z, far_place):
        pltpu.make_async_remote_copy(
            src_ref=outgoing.at[far_z * RIGHT + far_place],
            dst_ref=incoming.at[here],
            send_sem=send_sem.at[chunk],
            recv_sem=recv_sem.at[chunk],
            device_id=(far_z, core, far_place),
            device_id_type=MESH,
        ).start()

    def self_copy(outgoing, incoming, chunk):
        return pltpu.make_async_copy(
            outgoing.at[here], incoming.at[here], self_sem.at[chunk]
        )

    mix = exchange(4, 64)

    def pack(outgoing, chunk, count):
        def quarter(far_z, carry):
            def block(k):
                source = sources[chunk * 2 + k // 2, k % 2 * CHIPS + here]
                return both[source // ITEMS * depth + source % ITEMS, far_z]

            blocks = [block(k) for k in range(count)]
            if count == 2:
                blocks = [rows[:, : B // 2] for rows in blocks] + [rows[:, B // 2 :] for rows in blocks]
            rows = reorder(mix, jnp.concatenate(blocks, axis=0))
            outgoing[pl.ds(far_z * RIGHT, RIGHT)] = rows.reshape(
                RIGHT, 4 * ROWS, rows.shape[-1]
            )
            return carry

        lax.fori_loop(0, CHIPS_Z, quarter, 0)

    def stage(chunk, carry):
        @pl.when(chunk < stages)
        def _():
            lax.fori_loop(4 * chunk, 4 * chunk + 4, multiply, 0)
            lax.fori_loop(4 * chunk, 4 * chunk + 4, arrive, 0)

        pack(send.at[chunk], chunk, 4)

        @pl.when(chunk < stages - 1)
        def _():
            pl.semaphore_signal(free_sem, inc=1, device_id=partner, device_id_type=MESH)

        self_copy(send.at[chunk], arrived.at[chunk], chunk).start()
        for_others(functools.partial(departing, send.at[chunk], arrived.at[chunk], chunk))
        return carry

    lax.fori_loop(0, fours, stage, 0)
    if ends_in_pair:
        pack(send_pair, fours, 2)
        self_copy(send_pair, arrived_pair, fours).start()
        for_others(functools.partial(departing, send_pair, arrived_pair, fours))

    unsort = exchange(16, 16)

    def receive(outgoing, incoming, chunk, count, sorted_rows):
        self_copy(outgoing, incoming, chunk).wait()
        arrivals = incoming.at[pl.ds(0, CHIPS - 1)]
        pltpu.make_async_copy(arrivals, arrivals, recv_sem.at[chunk]).wait()

        def sort(far_z, carry):
            rows = incoming[pl.ds(far_z * RIGHT, RIGHT)]
            rows = reorder(unsort, rows.reshape(256, rows.shape[-1]))
            for piece in range(16):
                start = pl.multiple_of(piece % count * CHIPS + far_z * RIGHT, RIGHT)
                sorted_rows[piece // count, pl.ds(start, RIGHT), :] = rows[
                    piece * RIGHT : (piece + 1) * RIGHT
                ]
            return carry

        lax.fori_loop(0, CHIPS_Z, sort, 0)

    partial[...] = jnp.zeros(partial.shape, partial.dtype)
    placed = fours if ends_in_pair else fours - 1

    def collect(chunk, carry):
        receive(send.at[chunk], arrived.at[chunk], chunk, 4, ordered)

        @pl.when(chunk < placed)
        def _():
            label = label_of(labels, chunk * 4, 4)

            def put(part, carry):
                onehot = onehot_rows(label, part * 256, (256, 4 * CHIPS))

                def row(x, carry):
                    total = jnp.dot(
                        onehot, ordered[x], preferred_element_type=jnp.float32
                    ).reshape(8, SECTORS, B)
                    total = total + partial[pl.ds(part * 8, 8), x].astype(jnp.float32)
                    partial[pl.ds(part * 8, 8), x] = total.astype(jnp.bfloat16)
                    return carry

                return lax.fori_loop(0, ROWS, row, carry, unroll=2)

            lax.fori_loop(0, SECTORS // 8, put, 0)

        @pl.when(chunk == placed - 1)
        def _():
            pltpu.make_async_copy(partial, out, out_sem.at[0]).start()

        return carry

    lax.fori_loop(0, fours, collect, 0)
    rest = ordered
    if ends_in_pair:
        receive(send_pair, arrived_pair, fours, 2, ordered_pair)
        rest = ordered_pair
    rest_out = pltpu.make_async_copy(rest, last, out_sem.at[1])
    rest_out.start()

    def sent(rank, carry):
        pair_copy(rank).wait_send()
        return carry

    lax.fori_loop(0, depth, sent, 0)

    def gone(chunk, carry):
        departures = send.at[chunk, pl.ds(0, CHIPS - 1)]
        pltpu.make_async_copy(departures, departures, send_sem.at[chunk]).wait()
        return carry

    lax.fori_loop(0, fours, gone, 0)
    if ends_in_pair:
        departures = send_pair.at[pl.ds(0, CHIPS - 1)]
        pltpu.make_async_copy(departures, departures, send_sem.at[fours]).wait()
    pltpu.make_async_copy(partial, out, out_sem.at[0]).wait()
    rest_out.wait()


def exchanged(depth, slots, items, sources, labels, psi, env_left, env_right):
    smem = pl.BlockSpec(memory_space=pltpu.SMEM)
    anywhere = pl.BlockSpec(memory_space=pl.ANY)
    vmem = pl.BlockSpec(memory_space=pltpu.VMEM)
    bf16 = jnp.bfloat16
    fours = slots // 4
    messages = (CHIPS, 4 * ROWS, B)
    pair_messages = (CHIPS, 4 * ROWS, B // 2)
    dma = pltpu.SemaphoreType.DMA
    return pl.pallas_call(
        functools.partial(exchange_kernel, depth, slots),
        name=f"exchange_{slots}",
        out_shape=[
            jax.ShapeDtypeStruct((SECTORS, ROWS, SECTORS, B), bf16),
            jax.ShapeDtypeStruct(last_shape(last_count(slots)), bf16),
        ],
        in_specs=[smem] * 2 + [vmem] + [anywhere] * 3,
        out_specs=[anywhere] * 2,
        scratch_shapes=[
            pltpu.VMEM((LEFT_DEV, B * RIGHT_DEV, B), bf16),
            pltpu.VMEM((LEFT_DEV * RIGHT_DEV, B, B), bf16),
            pltpu.VMEM((TERMS * LEFT_DEV, B, B), bf16),
            pltpu.VMEM((TERMS * RIGHT_DEV, B, B), bf16),
            pltpu.VMEM((depth, CHIPS_Z, CORES, B // (CHIPS_Z * CORES), B), bf16),
            pltpu.VMEM((CORES * depth, CHIPS_Z, B // (CHIPS_Z * CORES), B), bf16),
            pltpu.VMEM((fours, *messages), bf16),
            pltpu.VMEM((fours, *messages), bf16),
            pltpu.VMEM(pair_messages, bf16),
            pltpu.VMEM(pair_messages, bf16),
            pltpu.VMEM((SECTORS, ROWS, SECTORS, B), bf16),
            pltpu.VMEM(last_shape(4), bf16),
            pltpu.VMEM(last_shape(2), bf16),
            dma((LEFT_DEV + 2,)),
            dma((depth,)),
            dma((depth,)),
            dma((depth,)),
            pltpu.SemaphoreType.REGULAR,
            dma((fours + 1,)),
            dma((fours + 1,)),
            dma((fours + 1,)),
            dma((2,)),
        ],
        compiler_params=pltpu.CompilerParams(
            collective_id=slots // 2,
            has_side_effects=True,
            vmem_limit_bytes=VMEM_LIMIT,
        ),
        cost_estimate=pl.CostEstimate(
            flops=4 * depth * B**3, bytes_accessed=14 * 2**20, transcendentals=0
        ),
    )(
        items,
        sources,
        labels,
        psi,
        env_left.reshape(TERMS * LEFT_DEV, B, B),
        env_right.reshape(TERMS * RIGHT_DEV, B, B),
    )


def finish_kernel(first, count, labels, partial, last, out, onehot):
    @pl.when((pl.program_id(0) == 0) & (pl.program_id(1) == 0))
    def _():
        label = label_of(labels, first, count)

        def build(part, carry):
            onehot[pl.ds(pl.multiple_of(part * 256, 256), 256), :] = onehot_rows(
                label, part * 256, (256, count * CHIPS)
            )
            return carry

        lax.fori_loop(0, SECTORS * SECTORS // 256, build, 0)

    def put(part, carry):
        total = jnp.dot(
            onehot[pl.ds(pl.multiple_of(part * 256, 256), 256), :],
            last[0],
            preferred_element_type=jnp.float32,
        ).reshape(8, SECTORS, last.shape[-1])
        old = partial[pl.ds(part * 8, 8), 0].astype(jnp.float32)
        out[pl.ds(part * 8, 8), 0] = (total + old).astype(jnp.bfloat16)
        return carry

    lax.fori_loop(0, SECTORS // 8, put, 0, unroll=2)


def finished(slots, labels, partial, last):
    count = last_count(slots)
    pieces, height, width = last_shape(count)
    halves = B // width
    block = pl.BlockSpec((SECTORS, 1, SECTORS, width), lambda x, w: (0, x, 0, w))
    return pl.pallas_call(
        functools.partial(finish_kernel, slots - count, count),
        name=f"finish_{slots}",
        grid=(ROWS, halves),
        out_shape=jax.ShapeDtypeStruct((SECTORS, ROWS, SECTORS, B), jnp.bfloat16),
        in_specs=[
            pl.BlockSpec((ITEMS, 128), lambda x, w: (0, 0)),
            block,
            pl.BlockSpec((1, height, width), lambda x, w: (x * halves + w, 0, 0)),
        ],
        out_specs=block,
        scratch_shapes=[pltpu.VMEM((SECTORS * SECTORS, height), jnp.bfloat16)],
        compiler_params=pltpu.CompilerParams(vmem_limit_bytes=VMEM_LIMIT),
        cost_estimate=pl.CostEstimate(
            flops=2 * SECTORS**2 * count * CHIPS * ROWS * B,
            bytes_accessed=9 * 2**20,
            transcendentals=0,
        ),
    )(labels, partial, last)


def local(psi, env_left, env_right, left_target, right_target, qn_left, qn_right):
    items, sources, labels, choice = tables(left_target, right_target, qn_left, qn_right)

    def branch(depth, slots, operands):
        labels = operands[2]
        return finished(slots, labels, *exchanged(depth, slots, *operands))

    return lax.switch(
        choice[0, 0],
        [functools.partial(branch, depth, slots) for depth, slots in SIZES],
        (items, sources, labels, psi, env_left, env_right),
    )


def solution(mesh):
    fine = Mesh(
        mesh.devices.reshape(CHIPS_Z, CORES, RIGHT), ("z", "core", "right")
    )
    left = ("z", "core")
    return jax.shard_map(
        local,
        mesh=fine,
        in_specs=(
            P(left, None, "right", None),
            P(None, left, None, None),
            P(None, "right", None, None),
            P(),
            P(),
            P(),
            P(),
        ),
        out_specs=P(None, ("z", "core", "right"), None, None),
        check_vma=False,
    )
```

```python
import functools

import jax
import jax.numpy as jnp
from jax import lax
from jax.experimental import pallas as pl
from jax.experimental.pallas import tpu as pltpu
from jax.sharding import Mesh, PartitionSpec as P

filling_charge = 3
B = 512
SECTORS = 32
TERMS = 2
CHIPS_Z = 4
CORES = 2
RIGHT = 16
CHIPS = CHIPS_Z * RIGHT
LEFT_DEV = SECTORS // (CHIPS_Z * CORES)
RIGHT_DEV = SECTORS // RIGHT
ITEMS = TERMS * LEFT_DEV * RIGHT_DEV
HALF = B // CORES
ROWS = B // (CHIPS * CORES)
MESH = pl.DeviceIdType.MESH
VMEM_LIMIT = 60 * 2**20
SIZES = ((10, 12), (10, 14), (12, 16), (12, 18), (16, 32))


def table_kernel(left_target, right_target, qn_left, qn_right, items, sources, labels, most):
    f32, bf16 = jnp.float32, jnp.bfloat16
    square = (SECTORS, SECTORS)
    row = lax.broadcasted_iota(jnp.int32, square, 0)
    column = lax.broadcasted_iota(jnp.int32, square, 1)
    wide = lambda value: value.astype(f32)
    dot = lambda a, b: jnp.dot(a.astype(bf16), b.astype(bf16), preferred_element_type=f32)
    upright = lambda line: jnp.sum(
        jnp.where(row == column, wide(line), 0.0), axis=1, keepdims=True
    )
    charge_left = qn_left[...]
    charge_right = upright(qn_right[...])

    pair = wide(row // RIGHT_DEV == column // RIGHT_DEV)
    second = wide((row + 1 == column) & (column % RIGHT_DEV == 1))
    same = row // LEFT_DEV == column // LEFT_DEV
    core = wide(row // LEFT_DEV % CORES)
    swap = wide(column == row + LEFT_DEV - 2 * LEFT_DEV * (row // LEFT_DEV % CORES))
    active, to_left, to_right, rank, total = [], [], [], [], []
    for t in range(TERMS):
        lefts = upright(left_target[t : t + 1, :])
        rights = wide(right_target[t : t + 1, :])
        hit_left = wide(column) == lefts
        hit_right = wide(row) == rights
        have_left = jnp.sum(jnp.where(hit_left, wide(charge_left), 0.0), axis=1, keepdims=True)
        have_right = jnp.sum(jnp.where(hit_right, charge_right, 0.0), axis=0, keepdims=True)
        allowed = have_left + have_right == float(filling_charge)
        ones = jnp.where(allowed, 1.0, 0.0)
        count = dot(ones, pair)
        active.append(allowed)
        to_left.append(lefts)
        to_right.append(rights)
        rank.append(dot(wide(same & (column < row)), count) + dot(ones, second))
        total.append(dot(wide(same), count))
    rank[1] = rank[1] + total[0]
    own = total[0] + total[1]
    other = dot(swap, own)
    slot = [r + jnp.minimum(other, r + core) for r in rank]

    lane = lax.broadcasted_iota(jnp.int32, (SECTORS, 128), 1)
    tall = lax.broadcasted_iota(jnp.int32, (SECTORS, 128), 0)
    device_lane = tall // RIGHT_DEV == lane % RIGHT
    device_row = tall // LEFT_DEV == lane // RIGHT
    chip_row = tall // (CORES * LEFT_DEV) == lane % CHIPS // RIGHT

    def spread(steps, place, values, rows):
        stack = []
        for k in steps:
            picked = jnp.zeros(square, f32)
            for t in range(TERMS):
                picked = picked + jnp.where(
                    active[t] & (place[t] == float(k)), values[t], 0.0
                )
            stack.append(picked.astype(bf16))
        lanes = dot(jnp.concatenate(stack, axis=0), wide(device_lane))
        lanes = lanes.reshape(len(stack), SECTORS, 128)
        return jnp.sum(jnp.where(rows[None], lanes, 0.0), axis=1)

    item = wide(row % LEFT_DEV * RIGHT_DEV + column % RIGHT_DEV)
    items[...] = spread(
        range(ITEMS), rank, [item, item + float(LEFT_DEV * RIGHT_DEV)], device_row
    ).astype(jnp.int32)

    half_lane = lax.broadcasted_iota(jnp.int32, (ITEMS, 128), 1)

    def by_slot(values):
        both = spread(
            [*range(0, 2 * ITEMS, 2), *range(1, 2 * ITEMS, 2)], slot, values, chip_row
        )
        return jnp.where(half_lane < CHIPS, both[:ITEMS], both[ITEMS:])

    sources[...] = by_slot([core * ITEMS + r for r in rank]).astype(jnp.int32)
    full = jnp.zeros(square, f32)
    high = by_slot([full + lefts + 1.0 for lefts in to_left])
    low = by_slot([full + rights for rights in to_right])
    labels[...] = ((high - 1.0) * SECTORS + low).astype(jnp.int32)
    most_device = jnp.max(own)
    most_chip = jnp.max(own + other)
    choice = jnp.int32(0)
    for depth, slots in SIZES[:-1]:
        choice = choice + jnp.where(
            (most_device > float(depth)) | (most_chip > float(slots)), 1, 0
        )
    most[0, 0] = choice


def tables(left_target, right_target, qn_left, qn_right):
    vmem = pl.BlockSpec(memory_space=pltpu.VMEM)
    table = jax.ShapeDtypeStruct((ITEMS, 128), jnp.int32)
    return pl.pallas_call(
        table_kernel,
        name="tables",
        out_shape=[table, table, table, jax.ShapeDtypeStruct((1, 1), jnp.int32)],
        in_specs=[vmem] * 4,
        out_specs=[vmem] * 3 + [pl.BlockSpec(memory_space=pltpu.SMEM)],
        cost_estimate=pl.CostEstimate(flops=2**24, bytes_accessed=2**15, transcendentals=0),
    )(
        left_target,
        right_target,
        qn_left.reshape(1, SECTORS),
        qn_right.reshape(1, SECTORS),
    )


def last_count(slots):
    return 2 if slots % 4 else 4


def last_shape(count):
    return ROWS * 4 // count, count * CHIPS, B * count // 4


def onehot_rows(label, first, shape):
    row = first + lax.broadcasted_iota(jnp.int32, shape, 0)
    return jnp.where(row == label, 1.0, 0.0).astype(jnp.bfloat16)


def label_of(labels, first, count):
    return jnp.concatenate(
        [labels[pl.ds(first // 2 + p, 1), :] for p in range(count // 2)], axis=1
    )


def exchange_kernel(
    depth,
    slots,
    items,
    sources,
    labels,
    psi_hbm,
    left_hbm,
    right_hbm,
    out,
    last,
    landed,
    psi,
    left,
    right,
    product,
    both,
    send,
    arrived,
    send_pair,
    arrived_pair,
    partial,
    ordered,
    ordered_pair,
    in_sem,
    own_sem,
    pair_send_sem,
    pair_recv_sem,
    free_sem,
    self_sem,
    send_sem,
    recv_sem,
    out_sem,
):
    z = lax.axis_index("z")
    core = lax.axis_index("core")
    place = lax.axis_index("right")
    other = 1 - core
    partner = (z, other, place)
    here = z * RIGHT + place
    device = (z * CORES + core) * RIGHT + place
    fours = slots // 4
    stages = -(-depth // 4)
    ends_in_pair = slots % 4 == 2

    psi_rows = psi_hbm.reshape(LEFT_DEV, B * RIGHT_DEV, B)
    psi_load = [
        pltpu.make_async_copy(psi_rows.at[a], landed.at[a], in_sem.at[a])
        for a in range(LEFT_DEV)
    ]
    left_load = pltpu.make_async_copy(left_hbm, left, in_sem.at[LEFT_DEV])
    right_load = pltpu.make_async_copy(right_hbm, right, in_sem.at[LEFT_DEV + 1])
    for load in psi_load:
        load.start()

    steps = (1, 3, 2, 0)
    route = []
    for i in range(RIGHT):
        step_x = steps[i % 4]
        step_y = steps[(i + i // 4) % 4]
        far_place = (place // 4 + step_x) % 4 * 4 + (place % 4 + step_y) % 4
        route.append((step_x + step_y, steps[(i + i // 4 * 2) % 4], far_place))

    def some_others(visit, first, last):
        def turn(shift):
            far_z = [(z + shift + step) % CHIPS_Z for step in range(CHIPS_Z)]
            for moved, step, far_place in route[first:last]:
                if moved or step:
                    visit(far_z[step], far_place)
                else:
                    pl.when(shift > 0)(functools.partial(visit, far_z[step], far_place))

        return turn

    def for_others(visit, first=0, last=RIGHT):
        turn = some_others(visit, first, last)

        def turned(shift, carry):
            turn(shift)
            return carry

        lax.fori_loop(0, CHIPS_Z, turned, 0)

    barrier = pltpu.get_barrier_semaphore()
    pl.semaphore_signal(barrier, inc=1, device_id=partner, device_id_type=MESH)

    def greet(far_z, far_place):
        pl.semaphore_signal(
            barrier, inc=1, device_id=(far_z, core, far_place), device_id_type=MESH
        )

    for_others(greet)

    def exchange(shape_from, shape_to):
        row = lax.broadcasted_iota(jnp.int32, (256, 256), 0)
        column = lax.broadcasted_iota(jnp.int32, (256, 256), 1)
        source = row % shape_from * shape_to + row // shape_from
        return jnp.where(column == source, 1.0, 0.0).astype(jnp.bfloat16)

    def reorder(onehot, rows):
        return jnp.dot(onehot, rows, preferred_element_type=jnp.float32).astype(
            jnp.bfloat16
        )

    unmix = exchange(128, RIGHT_DEV)

    def split(a, carry):
        for part in range(B // 128):
            apart = reorder(unmix, landed[a, part * 256 : part * 256 + 256, :])
            for b in range(RIGHT_DEV):
                psi[a * RIGHT_DEV + b, part * 128 : part * 128 + 128, :] = apart[
                    b * 128 : (b + 1) * 128
                ]
        return carry

    psi_load[0].wait()
    left_load.start()
    right_load.start()
    split(0, 0)

    def next_split(a, carry):
        pltpu.make_async_copy(psi_rows.at[a], landed.at[a], in_sem.at[a]).wait()
        return split(a, carry)

    lax.fori_loop(1, LEFT_DEV, next_split, 0)
    left_load.wait()
    right_load.wait()

    def own_copy(rank):
        return pltpu.make_async_copy(
            product.at[rank, :, core], both.at[core * depth + rank], own_sem.at[rank]
        )

    def pair_copy(rank):
        return pltpu.make_async_remote_copy(
            src_ref=product.at[rank, :, other],
            dst_ref=both.at[core * depth + rank],
            send_sem=pair_send_sem.at[rank],
            recv_sem=pair_recv_sem.at[rank],
            device_id=partner,
            device_id_type=MESH,
        )

    def multiply(rank):
        item = items[rank, device]
        term = item // (LEFT_DEV * RIGHT_DEV)
        pair = item % (LEFT_DEV * RIGHT_DEV)
        half = jnp.dot(
            left[term * LEFT_DEV + pair // RIGHT_DEV],
            psi[pair],
            preferred_element_type=jnp.float32,
        ).astype(jnp.bfloat16)
        moved = lax.dot_general(
            half,
            right[term * RIGHT_DEV + pair % RIGHT_DEV],
            (((1,), (1,)), ((), ())),
            preferred_element_type=jnp.float32,
        ).astype(jnp.bfloat16)
        product[rank] = moved.reshape(CHIPS_Z, CORES, B // (CHIPS_Z * CORES), B)

    def swap(rank):
        pair_copy(rank).start()
        own_copy(rank).start()

    def arrive(rank, carry):
        own_copy(rank).wait()
        pair_copy(rank).wait_recv()
        return carry

    def departing(outgoing, incoming, chunk, far_z, far_place):
        pltpu.make_async_remote_copy(
            src_ref=outgoing.at[far_z * RIGHT + far_place],
            dst_ref=incoming.at[here],
            send_sem=send_sem.at[chunk],
            recv_sem=recv_sem.at[chunk],
            device_id=(far_z, core, far_place),
            device_id_type=MESH,
        ).start()

    def self_copy(outgoing, incoming, chunk):
        return pltpu.make_async_copy(
            outgoing.at[here], incoming.at[here], self_sem.at[chunk]
        )

    mix = exchange(4, 64)

    def pack(outgoing, chunk, count):
        def quarter(far_z, carry):
            def block(k):
                source = sources[chunk * 2 + k // 2, k % 2 * CHIPS + here]
                return both[source // ITEMS * depth + source % ITEMS, far_z]

            blocks = [block(k) for k in range(count)]
            if count == 2:
                blocks = [rows[:, : B // 2] for rows in blocks] + [rows[:, B // 2 :] for rows in blocks]
            rows = reorder(mix, jnp.concatenate(blocks, axis=0))
            outgoing[pl.ds(far_z * RIGHT, RIGHT)] = rows.reshape(
                RIGHT, 4 * ROWS, rows.shape[-1]
            )
            return carry

        lax.fori_loop(0, CHIPS_Z, quarter, 0, unroll=2)

    def leave(chunk):
        return functools.partial(departing, send.at[chunk], arrived.at[chunk], chunk)

    def packed(chunk, ready):
        lax.fori_loop(4 * chunk, ready, arrive, 0)
        pack(send.at[chunk], chunk, 4)

        @pl.when(chunk < stages - 1)
        def _():
            pl.semaphore_signal(free_sem, inc=1, device_id=partner, device_id_type=MESH)

        self_copy(send.at[chunk], arrived.at[chunk], chunk).start()

    def first(rank, carry):
        multiply(rank)

        @pl.when(rank == 0)
        def _():
            pl.semaphore_wait(barrier, CHIPS)

        swap(rank)
        return carry

    lax.fori_loop(0, 4, first, 0)
    packed(0, 4)

    def stage(chunk, carry):
        for_others(leave(chunk - 1), 0, 4)
        turn = some_others(leave(chunk - 1), 4, RIGHT)
        count = jnp.clip(depth - 4 * chunk, 0, 4)

        @pl.when(chunk < stages)
        def _():
            pl.semaphore_wait(free_sem, 1)

        def both_at_once(step, carry):
            turn(step)
            multiply(4 * chunk + step)
            swap(4 * chunk + step)
            return carry

        def send_only(step, carry):
            turn(step)
            return carry

        lax.fori_loop(0, count, both_at_once, 0)
        lax.fori_loop(count, CHIPS_Z, send_only, 0)
        packed(chunk, 4 * chunk + count)
        return carry

    lax.fori_loop(1, fours, stage, 0)
    for_others(leave(fours - 1))
    if ends_in_pair:
        pack(send_pair, fours, 2)
        self_copy(send_pair, arrived_pair, fours).start()
        for_others(functools.partial(departing, send_pair, arrived_pair, fours))

    unsort = exchange(16, 16)

    def receive(outgoing, incoming, chunk, count, sorted_rows):
        self_copy(outgoing, incoming, chunk).wait()
        arrivals = incoming.at[pl.ds(0, CHIPS - 1)]
        pltpu.make_async_copy(arrivals, arrivals, recv_sem.at[chunk]).wait()

        def sort(far_z, carry):
            rows = incoming[pl.ds(far_z * RIGHT, RIGHT)]
            rows = reorder(unsort, rows.reshape(256, rows.shape[-1]))
            for piece in range(16):
                start = pl.multiple_of(piece % count * CHIPS + far_z * RIGHT, RIGHT)
                sorted_rows[piece // count, pl.ds(start, RIGHT), :] = rows[
                    piece * RIGHT : (piece + 1) * RIGHT
                ]
            return carry

        lax.fori_loop(0, CHIPS_Z, sort, 0)

    partial[...] = jnp.zeros(partial.shape, partial.dtype)
    placed = fours if ends_in_pair else fours - 1

    def collect(chunk, carry):
        receive(send.at[chunk], arrived.at[chunk], chunk, 4, ordered)

        @pl.when(chunk < placed)
        def _():
            label = label_of(labels, chunk * 4, 4)

            def put(part, carry):
                onehot = onehot_rows(label, part * 256, (256, 4 * CHIPS))

                def row(x, carry):
                    total = jnp.dot(
                        onehot, ordered[x], preferred_element_type=jnp.float32
                    ).reshape(8, SECTORS, B)
                    total = total + partial[pl.ds(part * 8, 8), x].astype(jnp.float32)
                    partial[pl.ds(part * 8, 8), x] = total.astype(jnp.bfloat16)
                    return carry

                return lax.fori_loop(0, ROWS, row, carry, unroll=2)

            lax.fori_loop(0, SECTORS // 8, put, 0)

        @pl.when(chunk == placed - 1)
        def _():
            pltpu.make_async_copy(partial, out, out_sem.at[0]).start()

        return carry

    lax.fori_loop(0, fours, collect, 0)
    rest = ordered
    if ends_in_pair:
        receive(send_pair, arrived_pair, fours, 2, ordered_pair)
        rest = ordered_pair
    rest_out = pltpu.make_async_copy(rest, last, out_sem.at[1])
    rest_out.start()

    def sent(rank, carry):
        pair_copy(rank).wait_send()
        return carry

    lax.fori_loop(0, depth, sent, 0)

    def gone(chunk, carry):
        departures = send.at[chunk, pl.ds(0, CHIPS - 1)]
        pltpu.make_async_copy(departures, departures, send_sem.at[chunk]).wait()
        return carry

    lax.fori_loop(0, fours, gone, 0)
    if ends_in_pair:
        departures = send_pair.at[pl.ds(0, CHIPS - 1)]
        pltpu.make_async_copy(departures, departures, send_sem.at[fours]).wait()
    pltpu.make_async_copy(partial, out, out_sem.at[0]).wait()
    rest_out.wait()


def exchanged(depth, slots, items, sources, labels, psi, env_left, env_right):
    smem = pl.BlockSpec(memory_space=pltpu.SMEM)
    anywhere = pl.BlockSpec(memory_space=pl.ANY)
    vmem = pl.BlockSpec(memory_space=pltpu.VMEM)
    bf16 = jnp.bfloat16
    fours = slots // 4
    messages = (CHIPS, 4 * ROWS, B)
    pair_messages = (CHIPS, 4 * ROWS, B // 2)
    dma = pltpu.SemaphoreType.DMA
    return pl.pallas_call(
        functools.partial(exchange_kernel, depth, slots),
        name=f"exchange_{slots}",
        out_shape=[
            jax.ShapeDtypeStruct((SECTORS, ROWS, SECTORS, B), bf16),
            jax.ShapeDtypeStruct(last_shape(last_count(slots)), bf16),
        ],
        in_specs=[smem] * 2 + [vmem] + [anywhere] * 3,
        out_specs=[anywhere] * 2,
        scratch_shapes=[
            pltpu.VMEM((LEFT_DEV, B * RIGHT_DEV, B), bf16),
            pltpu.VMEM((LEFT_DEV * RIGHT_DEV, B, B), bf16),
            pltpu.VMEM((TERMS * LEFT_DEV, B, B), bf16),
            pltpu.VMEM((TERMS * RIGHT_DEV, B, B), bf16),
            pltpu.VMEM((depth, CHIPS_Z, CORES, B // (CHIPS_Z * CORES), B), bf16),
            pltpu.VMEM((CORES * depth, CHIPS_Z, B // (CHIPS_Z * CORES), B), bf16),
            pltpu.VMEM((fours, *messages), bf16),
            pltpu.VMEM((fours, *messages), bf16),
            pltpu.VMEM(pair_messages, bf16),
            pltpu.VMEM(pair_messages, bf16),
            pltpu.VMEM((SECTORS, ROWS, SECTORS, B), bf16),
            pltpu.VMEM(last_shape(4), bf16),
            pltpu.VMEM(last_shape(2), bf16),
            dma((LEFT_DEV + 2,)),
            dma((depth,)),
            dma((depth,)),
            dma((depth,)),
            pltpu.SemaphoreType.REGULAR,
            dma((fours + 1,)),
            dma((fours + 1,)),
            dma((fours + 1,)),
            dma((2,)),
        ],
        compiler_params=pltpu.CompilerParams(
            collective_id=slots // 2,
            has_side_effects=True,
            vmem_limit_bytes=VMEM_LIMIT,
        ),
        cost_estimate=pl.CostEstimate(
            flops=4 * depth * B**3, bytes_accessed=14 * 2**20, transcendentals=0
        ),
    )(
        items,
        sources,
        labels,
        psi,
        env_left.reshape(TERMS * LEFT_DEV, B, B),
        env_right.reshape(TERMS * RIGHT_DEV, B, B),
    )


def finish_kernel(first, count, labels, partial, last, out, held, rest, sem, rest_sem):
    parts = held.shape[0] // 8

    def fetch(part):
        rows = pl.ds(part * 8, 8)
        return pltpu.make_async_copy(partial.at[rows], held.at[rows], sem.at[part])

    def store(part):
        rows = pl.ds(part * 8, 8)
        return pltpu.make_async_copy(held.at[rows], out.at[rows], sem.at[part])

    rest_fetch = pltpu.make_async_copy(last, rest, rest_sem)
    rest_fetch.start()
    for part in range(parts):
        fetch(part).start()
    label = label_of(labels, first, count)
    rest_fetch.wait()

    def add(part, carry):
        onehot = onehot_rows(label, part * 256, (256, count * CHIPS))
        fetch(part).wait()
        width = rest.shape[-1]
        for piece in range(rest.shape[0]):
            x, lanes = piece * width // B, piece * width % B
            lanes = slice(lanes, lanes + width)
            total = jnp.dot(
                onehot, rest[piece], preferred_element_type=jnp.float32
            ).reshape(8, SECTORS, width)
            total = total + held[pl.ds(part * 8, 8), x, :, lanes].astype(jnp.float32)
            held[pl.ds(part * 8, 8), x, :, lanes] = total.astype(jnp.bfloat16)
        store(part).start()
        return carry

    lax.fori_loop(0, parts, add, 0)
    for part in range(parts):
        store(part).wait()


def finished(slots, labels, partial, last):
    count = last_count(slots)
    anywhere = pl.BlockSpec(memory_space=pl.ANY)
    return pl.pallas_call(
        functools.partial(finish_kernel, slots - count, count),
        name=f"finish_{slots}",
        out_shape=jax.ShapeDtypeStruct(partial.shape, partial.dtype),
        in_specs=[pl.BlockSpec(memory_space=pltpu.VMEM), anywhere, anywhere],
        out_specs=anywhere,
        scratch_shapes=[
            pltpu.VMEM(partial.shape, partial.dtype),
            pltpu.VMEM(last.shape, last.dtype),
            pltpu.SemaphoreType.DMA((SECTORS // 8,)),
            pltpu.SemaphoreType.DMA,
        ],
        compiler_params=pltpu.CompilerParams(vmem_limit_bytes=VMEM_LIMIT),
        cost_estimate=pl.CostEstimate(
            flops=2 * SECTORS**2 * count * CHIPS * ROWS * B,
            bytes_accessed=9 * 2**20,
            transcendentals=0,
        ),
    )(labels, partial, last)


def local(psi, env_left, env_right, left_target, right_target, qn_left, qn_right):
    items, sources, labels, choice = tables(left_target, right_target, qn_left, qn_right)

    def branch(depth, slots, operands):
        labels = operands[2]
        return finished(slots, labels, *exchanged(depth, slots, *operands))

    return lax.switch(
        choice[0, 0],
        [functools.partial(branch, depth, slots) for depth, slots in SIZES],
        (items, sources, labels, psi, env_left, env_right),
    )


def solution(mesh):
    fine = Mesh(
        mesh.devices.reshape(CHIPS_Z, CORES, RIGHT), ("z", "core", "right")
    )
    left = ("z", "core")
    return jax.shard_map(
        local,
        mesh=fine,
        in_specs=(
            P(left, None, "right", None),
            P(None, left, None, None),
            P(None, "right", None, None),
            P(),
            P(),
            P(),
            P(),
        ),
        out_specs=P(None, ("z", "core", "right"), None, None),
        check_vma=False,
    )
```

```python
import functools

import jax
import jax.numpy as jnp
from jax import lax
from jax.experimental import pallas as pl
from jax.experimental.pallas import tpu as pltpu
from jax.sharding import Mesh, PartitionSpec as P

filling_charge = 3
B = 512
SECTORS = 32
TERMS = 2
CHIPS_Z = 4
CORES = 2
RIGHT = 16
CHIPS = CHIPS_Z * RIGHT
LEFT_DEV = SECTORS // (CHIPS_Z * CORES)
RIGHT_DEV = SECTORS // RIGHT
ITEMS = TERMS * LEFT_DEV * RIGHT_DEV
HALF = B // CORES
ROWS = B // (CHIPS * CORES)
MESH = pl.DeviceIdType.MESH
VMEM_LIMIT = 60 * 2**20
SIZES = ((10, 12), (10, 14), (12, 16), (12, 18), (16, 32))


def table_kernel(left_target, right_target, qn_left, qn_right, items, sources, labels, most):
    f32, bf16 = jnp.float32, jnp.bfloat16
    square = (SECTORS, SECTORS)
    row = lax.broadcasted_iota(jnp.int32, square, 0)
    column = lax.broadcasted_iota(jnp.int32, square, 1)
    wide = lambda value: value.astype(f32)
    dot = lambda a, b: jnp.dot(a.astype(bf16), b.astype(bf16), preferred_element_type=f32)
    upright = lambda line: jnp.sum(
        jnp.where(row == column, wide(line), 0.0), axis=1, keepdims=True
    )
    charge_left = qn_left[...]
    charge_right = upright(qn_right[...])

    pair = wide(row // RIGHT_DEV == column // RIGHT_DEV)
    second = wide((row + 1 == column) & (column % RIGHT_DEV == 1))
    same = row // LEFT_DEV == column // LEFT_DEV
    core = wide(row // LEFT_DEV % CORES)
    swap = wide(column == row + LEFT_DEV - 2 * LEFT_DEV * (row // LEFT_DEV % CORES))
    active, to_left, to_right, rank, total = [], [], [], [], []
    for t in range(TERMS):
        lefts = upright(left_target[t : t + 1, :])
        rights = wide(right_target[t : t + 1, :])
        hit_left = wide(column) == lefts
        hit_right = wide(row) == rights
        have_left = jnp.sum(jnp.where(hit_left, wide(charge_left), 0.0), axis=1, keepdims=True)
        have_right = jnp.sum(jnp.where(hit_right, charge_right, 0.0), axis=0, keepdims=True)
        allowed = have_left + have_right == float(filling_charge)
        ones = jnp.where(allowed, 1.0, 0.0)
        count = dot(ones, pair)
        active.append(allowed)
        to_left.append(lefts)
        to_right.append(rights)
        rank.append(dot(wide(same & (column < row)), count) + dot(ones, second))
        total.append(dot(wide(same), count))
    rank[1] = rank[1] + total[0]
    own = total[0] + total[1]
    other = dot(swap, own)
    slot = [r + jnp.minimum(other, r + core) for r in rank]

    lane = lax.broadcasted_iota(jnp.int32, (SECTORS, 128), 1)
    tall = lax.broadcasted_iota(jnp.int32, (SECTORS, 128), 0)
    device_lane = tall // RIGHT_DEV == lane % RIGHT
    device_row = tall // LEFT_DEV == lane // RIGHT
    chip_row = tall // (CORES * LEFT_DEV) == lane % CHIPS // RIGHT

    def spread(steps, place, values, rows):
        stack = []
        for k in steps:
            picked = jnp.zeros(square, f32)
            for t in range(TERMS):
                picked = picked + jnp.where(
                    active[t] & (place[t] == float(k)), values[t], 0.0
                )
            stack.append(picked.astype(bf16))
        lanes = dot(jnp.concatenate(stack, axis=0), wide(device_lane))
        lanes = lanes.reshape(len(stack), SECTORS, 128)
        return jnp.sum(jnp.where(rows[None], lanes, 0.0), axis=1)

    item = wide(row % LEFT_DEV * RIGHT_DEV + column % RIGHT_DEV)
    items[...] = spread(
        range(ITEMS), rank, [item, item + float(LEFT_DEV * RIGHT_DEV)], device_row
    ).astype(jnp.int32)

    half_lane = lax.broadcasted_iota(jnp.int32, (ITEMS, 128), 1)

    def by_slot(values):
        both = spread(
            [*range(0, 2 * ITEMS, 2), *range(1, 2 * ITEMS, 2)], slot, values, chip_row
        )
        return jnp.where(half_lane < CHIPS, both[:ITEMS], both[ITEMS:])

    sources[...] = by_slot([core * ITEMS + r for r in rank]).astype(jnp.int32)
    full = jnp.zeros(square, f32)
    high = by_slot([full + lefts + 1.0 for lefts in to_left])
    low = by_slot([full + rights for rights in to_right])
    labels[...] = ((high - 1.0) * SECTORS + low).astype(jnp.int32)
    most_device = jnp.max(own)
    most_chip = jnp.max(own + other)
    choice = jnp.int32(0)
    for depth, slots in SIZES[:-1]:
        choice = choice + jnp.where(
            (most_device > float(depth)) | (most_chip > float(slots)), 1, 0
        )
    most[0, 0] = choice


def tables(left_target, right_target, qn_left, qn_right):
    vmem = pl.BlockSpec(memory_space=pltpu.VMEM)
    table = jax.ShapeDtypeStruct((ITEMS, 128), jnp.int32)
    return pl.pallas_call(
        table_kernel,
        name="tables",
        out_shape=[table, table, table, jax.ShapeDtypeStruct((1, 1), jnp.int32)],
        in_specs=[vmem] * 4,
        out_specs=[vmem] * 3 + [pl.BlockSpec(memory_space=pltpu.SMEM)],
        cost_estimate=pl.CostEstimate(flops=2**24, bytes_accessed=2**15, transcendentals=0),
    )(
        left_target,
        right_target,
        qn_left.reshape(1, SECTORS),
        qn_right.reshape(1, SECTORS),
    )


def fours_of(slots):
    return (slots - 2) // 4


def last_count(slots):
    return 4 if slots % 4 == 2 else 2


def last_shape(count):
    return ROWS * 4 // count, count * CHIPS, B * count // 4


def onehot_rows(label, first, shape):
    row = first + lax.broadcasted_iota(jnp.int32, shape, 0)
    return jnp.where(row == label, 1.0, 0.0).astype(jnp.bfloat16)


def label_of(labels, first, count):
    return jnp.concatenate(
        [labels[pl.ds(first // 2 + p, 1), :] for p in range(count // 2)], axis=1
    )


def exchange_kernel(
    depth,
    slots,
    items,
    sources,
    labels,
    psi_hbm,
    left_hbm,
    right_hbm,
    out,
    last,
    landed,
    psi,
    left,
    right,
    product,
    both,
    send,
    arrived,
    send_pair,
    arrived_pair,
    partial,
    ordered,
    ordered_pair,
    in_sem,
    own_sem,
    pair_send_sem,
    pair_recv_sem,
    free_sem,
    self_sem,
    send_sem,
    recv_sem,
    out_sem,
):
    z = lax.axis_index("z")
    core = lax.axis_index("core")
    place = lax.axis_index("right")
    other = 1 - core
    partner = (z, other, place)
    here = z * RIGHT + place
    device = (z * CORES + core) * RIGHT + place
    fours = fours_of(slots)
    stages = -(-(depth + 2) // 4)
    ends_in_pair = last_count(slots) == 2

    psi_rows = psi_hbm.reshape(LEFT_DEV, B * RIGHT_DEV, B)
    psi_load = [
        pltpu.make_async_copy(psi_rows.at[a], landed.at[a], in_sem.at[a])
        for a in range(LEFT_DEV)
    ]
    left_load = pltpu.make_async_copy(left_hbm, left, in_sem.at[LEFT_DEV])
    right_load = pltpu.make_async_copy(right_hbm, right, in_sem.at[LEFT_DEV + 1])
    for load in psi_load:
        load.start()

    steps = (1, 3, 2, 0)
    way = 1 - 2 * core
    route = []
    for i in range(RIGHT):
        step_x = steps[i % 4]
        step_y = steps[(i + i // 4) % 4]
        far_x = (place // 4 + 4 + way * step_x) % 4
        far_y = (place % 4 + 4 + way * step_y) % 4
        route.append((step_x + step_y, steps[(i + i // 4 * 2) % 4], far_x * 4 + far_y))

    def for_others(visit):
        def turn(shift, carry):
            far_z = [
                (z + 2 * CHIPS_Z + way * (shift + step)) % CHIPS_Z for step in range(CHIPS_Z)
            ]
            for moved, step, far_place in route:
                if moved or step:
                    visit(far_z[step], far_place)
                else:
                    pl.when(shift > 0)(functools.partial(visit, far_z[step], far_place))
            return carry

        lax.fori_loop(0, CHIPS_Z, turn, 0)

    barrier = pltpu.get_barrier_semaphore()
    pl.semaphore_signal(barrier, inc=1, device_id=partner, device_id_type=MESH)

    def greet(far_z, far_place):
        pl.semaphore_signal(
            barrier, inc=1, device_id=(far_z, core, far_place), device_id_type=MESH
        )

    for_others(greet)

    def exchange(shape_from, shape_to):
        row = lax.broadcasted_iota(jnp.int32, (256, 256), 0)
        column = lax.broadcasted_iota(jnp.int32, (256, 256), 1)
        source = row % shape_from * shape_to + row // shape_from
        return jnp.where(column == source, 1.0, 0.0).astype(jnp.bfloat16)

    def reorder(onehot, rows):
        return jnp.dot(onehot, rows, preferred_element_type=jnp.float32).astype(
            jnp.bfloat16
        )

    unmix = exchange(128, RIGHT_DEV)

    def split(a, carry):
        for part in range(B // 128):
            apart = reorder(unmix, landed[a, part * 256 : part * 256 + 256, :])
            for b in range(RIGHT_DEV):
                psi[a * RIGHT_DEV + b, part * 128 : part * 128 + 128, :] = apart[
                    b * 128 : (b + 1) * 128
                ]
        return carry

    psi_load[0].wait()
    left_load.start()
    right_load.start()
    split(0, 0)

    def next_split(a, carry):
        pltpu.make_async_copy(psi_rows.at[a], landed.at[a], in_sem.at[a]).wait()
        return split(a, carry)

    lax.fori_loop(1, LEFT_DEV, next_split, 0)
    left_load.wait()
    right_load.wait()

    def own_copy(rank):
        return pltpu.make_async_copy(
            product.at[rank, :, core], both.at[core * depth + rank], own_sem.at[rank]
        )

    def pair_copy(rank):
        return pltpu.make_async_remote_copy(
            src_ref=product.at[rank, :, other],
            dst_ref=both.at[core * depth + rank],
            send_sem=pair_send_sem.at[rank],
            recv_sem=pair_recv_sem.at[rank],
            device_id=partner,
            device_id_type=MESH,
        )

    def multiply(rank, carry):
        item = items[rank, device]
        term = item // (LEFT_DEV * RIGHT_DEV)
        pair = item % (LEFT_DEV * RIGHT_DEV)
        half = jnp.dot(
            left[term * LEFT_DEV + pair // RIGHT_DEV],
            psi[pair],
            preferred_element_type=jnp.float32,
        ).astype(jnp.bfloat16)
        moved = lax.dot_general(
            half,
            right[term * RIGHT_DEV + pair % RIGHT_DEV],
            (((1,), (1,)), ((), ())),
            preferred_element_type=jnp.float32,
        ).astype(jnp.bfloat16)
        product[rank] = moved.reshape(CHIPS_Z, CORES, B // (CHIPS_Z * CORES), B)

        @pl.when(rank == 0)
        def _():
            pl.semaphore_wait(barrier, CHIPS)

        @pl.when((rank > 0) & (rank % 4 == 2))
        def _():
            pl.semaphore_wait(free_sem, 1)

        pair_copy(rank).start()
        own_copy(rank).start()
        return carry

    def arrive(rank, carry):
        own_copy(rank).wait()
        pair_copy(rank).wait_recv()
        return carry

    def depart(outgoing, incoming, chunk, part=()):
        pltpu.make_async_copy(
            outgoing.at[here, *part], incoming.at[here, *part], self_sem.at[chunk]
        ).start()

        def start(far_z, far_place):
            pltpu.make_async_remote_copy(
                src_ref=outgoing.at[far_z * RIGHT + far_place, *part],
                dst_ref=incoming.at[here, *part],
                send_sem=send_sem.at[chunk],
                recv_sem=recv_sem.at[chunk],
                device_id=(far_z, core, far_place),
                device_id_type=MESH,
            ).start()

        for_others(start)

    def self_wait(outgoing, incoming, chunk, part=()):
        pltpu.make_async_copy(
            outgoing.at[here, *part], incoming.at[here, *part], self_sem.at[chunk]
        ).wait()

    def others_wait(buffer, sem, part=()):
        others = buffer.at[pl.ds(0, CHIPS - 1), *part]
        pltpu.make_async_copy(others, others, sem).wait()

    def seat(four):
        return (four + 1) // 2, (four + 1) % 2

    def for_message(four, visit):
        message, half = seat(four)
        single = (four == 0) | ((four == fours - 1) & (half == 0))
        pl.when(single)(lambda: visit(message, (half,)))
        pl.when((half == 1) & (four > 0))(lambda: visit(message, ()))

    def for_first(four, visit):
        message, half = seat(four)
        single = (four == 0) | ((four == fours - 1) & (half == 0))
        pl.when(single)(lambda: visit(message, (half,)))
        pl.when((half == 0) & (four < fours - 1))(lambda: visit(message, ()))

    mix = exchange(4, 64)

    def pack(outgoing, first, count, part=()):
        def quarter(far_z, carry):
            def block(k):
                source = sources[first // 2 + k // 2, k % 2 * CHIPS + here]
                return both[source // ITEMS * depth + source % ITEMS, far_z]

            blocks = [block(k) for k in range(count)]
            if count == 2:
                blocks = [rows[:, : B // 2] for rows in blocks] + [rows[:, B // 2 :] for rows in blocks]
            rows = reorder(mix, jnp.concatenate(blocks, axis=0))
            outgoing[pl.ds(far_z * RIGHT, RIGHT), *part] = rows.reshape(
                RIGHT, 4 * ROWS, rows.shape[-1]
            )
            return carry

        lax.fori_loop(0, CHIPS_Z, quarter, 0, unroll=2)

    messages = send.shape[0]

    def stage(turn, carry):
        start = jnp.maximum(4 * turn - 2, 0)
        stop = jnp.maximum(jnp.minimum(4 * turn + 2, depth), start)
        lax.fori_loop(start, stop, multiply, 0)
        lax.fori_loop(start, stop, arrive, 0)

        @pl.when(turn == 0)
        def _():
            pack(send_pair.at[0], 0, 2)
            depart(send_pair.at[0], arrived_pair.at[0], messages)

        @pl.when(turn > 0)
        def _():
            four = turn - 1
            message, half = seat(four)
            pack(send.at[message], 2 + 4 * four, 4, (half,))
            for_message(
                four,
                lambda message, part: depart(
                    send.at[message], arrived.at[message], message, part
                ),
            )

        @pl.when(turn < stages - 1)
        def _():
            pl.semaphore_signal(free_sem, inc=1, device_id=partner, device_id_type=MESH)

        return carry

    lax.fori_loop(0, fours + 1, stage, 0)
    if ends_in_pair:
        pack(send_pair.at[1], slots - 2, 2)
        depart(send_pair.at[1], arrived_pair.at[1], messages + 1)

    unsort = exchange(16, 16)

    def receive(outgoing, incoming, chunk, part=()):
        self_wait(outgoing, incoming, chunk, part)
        others_wait(incoming, recv_sem.at[chunk], part)

    def ordering(incoming, count, sorted_rows, part=()):
        def sort(far_z, carry):
            rows = incoming[pl.ds(far_z * RIGHT, RIGHT), *part]
            rows = reorder(unsort, rows.reshape(256, rows.shape[-1]))
            for piece in range(16):
                start = pl.multiple_of(piece % count * CHIPS + far_z * RIGHT, RIGHT)
                sorted_rows[piece // count, pl.ds(start, RIGHT), :] = rows[
                    piece * RIGHT : (piece + 1) * RIGHT
                ]
            return carry

        lax.fori_loop(0, CHIPS_Z, sort, 0)

    partial[...] = jnp.zeros(partial.shape, partial.dtype)

    def place_chunk(first, count, sorted_rows):
        label = label_of(labels, first, count)
        pieces, _, width = sorted_rows.shape

        def put(part, carry):
            onehot = onehot_rows(label, part * 256, (256, count * CHIPS))

            def row(x, carry):
                for half in range(pieces // ROWS):
                    lanes = slice(half * width, half * width + width)
                    total = jnp.dot(
                        onehot,
                        sorted_rows[x * (pieces // ROWS) + half],
                        preferred_element_type=jnp.float32,
                    ).reshape(8, SECTORS, width)
                    total = total + partial[pl.ds(part * 8, 8), x, :, lanes].astype(jnp.float32)
                    partial[pl.ds(part * 8, 8), x, :, lanes] = total.astype(jnp.bfloat16)
                return carry

            return lax.fori_loop(0, ROWS, row, carry, unroll=2)

        lax.fori_loop(0, SECTORS // 8, put, 0)

    receive(send_pair.at[0], arrived_pair.at[0], messages)
    ordering(arrived_pair.at[0], 2, ordered_pair)
    place_chunk(0, 2, ordered_pair)
    placed = fours if ends_in_pair else fours - 1

    def collect(four, carry):
        for_first(
            four,
            lambda message, part: receive(
                send.at[message], arrived.at[message], message, part
            ),
        )
        message, half = seat(four)
        ordering(arrived.at[message], 4, ordered, (half,))

        @pl.when(four < placed)
        def _():
            place_chunk(2 + 4 * four, 4, ordered)

        @pl.when(four == placed - 1)
        def _():
            pltpu.make_async_copy(partial, out, out_sem.at[0]).start()

        return carry

    lax.fori_loop(0, fours, collect, 0)
    rest = ordered
    if ends_in_pair:
        receive(send_pair.at[1], arrived_pair.at[1], messages + 1)
        ordering(arrived_pair.at[1], 2, ordered_pair)
        rest = ordered_pair
    rest_out = pltpu.make_async_copy(rest, last, out_sem.at[1])
    rest_out.start()

    def sent(rank, carry):
        pair_copy(rank).wait_send()
        return carry

    lax.fori_loop(0, depth, sent, 0)

    def gone(four, carry):
        for_message(
            four,
            lambda message, part: others_wait(send.at[message], send_sem.at[message], part),
        )
        return carry

    lax.fori_loop(0, fours, gone, 0)
    for pair in range(1 + ends_in_pair):
        others_wait(send_pair.at[pair], send_sem.at[messages + pair])
    pltpu.make_async_copy(partial, out, out_sem.at[0]).wait()
    rest_out.wait()


def exchanged(depth, slots, items, sources, labels, psi, env_left, env_right):
    smem = pl.BlockSpec(memory_space=pltpu.SMEM)
    anywhere = pl.BlockSpec(memory_space=pl.ANY)
    vmem = pl.BlockSpec(memory_space=pltpu.VMEM)
    bf16 = jnp.bfloat16
    fours = fours_of(slots)
    messages = fours // 2 + 1
    message = (CHIPS, 2, 4 * ROWS, B)
    pair_messages = (2, CHIPS, 4 * ROWS, B // 2)
    dma = pltpu.SemaphoreType.DMA
    return pl.pallas_call(
        functools.partial(exchange_kernel, depth, slots),
        name=f"exchange_{slots}",
        out_shape=[
            jax.ShapeDtypeStruct((SECTORS, ROWS, SECTORS, B), bf16),
            jax.ShapeDtypeStruct(last_shape(last_count(slots)), bf16),
        ],
        in_specs=[smem] * 2 + [vmem] + [anywhere] * 3,
        out_specs=[anywhere] * 2,
        scratch_shapes=[
            pltpu.VMEM((LEFT_DEV, B * RIGHT_DEV, B), bf16),
            pltpu.VMEM((LEFT_DEV * RIGHT_DEV, B, B), bf16),
            pltpu.VMEM((TERMS * LEFT_DEV, B, B), bf16),
            pltpu.VMEM((TERMS * RIGHT_DEV, B, B), bf16),
            pltpu.VMEM((depth, CHIPS_Z, CORES, B // (CHIPS_Z * CORES), B), bf16),
            pltpu.VMEM((CORES * depth, CHIPS_Z, B // (CHIPS_Z * CORES), B), bf16),
            pltpu.VMEM((messages, *message), bf16),
            pltpu.VMEM((messages, *message), bf16),
            pltpu.VMEM(pair_messages, bf16),
            pltpu.VMEM(pair_messages, bf16),
            pltpu.VMEM((SECTORS, ROWS, SECTORS, B), bf16),
            pltpu.VMEM(last_shape(4), bf16),
            pltpu.VMEM(last_shape(2), bf16),
            dma((LEFT_DEV + 2,)),
            dma((depth,)),
            dma((depth,)),
            dma((depth,)),
            pltpu.SemaphoreType.REGULAR,
            dma((messages + 2,)),
            dma((messages + 2,)),
            dma((messages + 2,)),
            dma((2,)),
        ],
        compiler_params=pltpu.CompilerParams(
            collective_id=slots // 2,
            has_side_effects=True,
            vmem_limit_bytes=VMEM_LIMIT,
        ),
        cost_estimate=pl.CostEstimate(
            flops=4 * depth * B**3, bytes_accessed=14 * 2**20, transcendentals=0
        ),
    )(
        items,
        sources,
        labels,
        psi,
        env_left.reshape(TERMS * LEFT_DEV, B, B),
        env_right.reshape(TERMS * RIGHT_DEV, B, B),
    )


def finish_kernel(first, count, labels, partial, last, out, held, rest, sem, rest_sem):
    parts = held.shape[0] // 8

    def fetch(part):
        rows = pl.ds(part * 8, 8)
        return pltpu.make_async_copy(partial.at[rows], held.at[rows], sem.at[part])

    def store(part):
        rows = pl.ds(part * 8, 8)
        return pltpu.make_async_copy(held.at[rows], out.at[rows], sem.at[part])

    rest_fetch = pltpu.make_async_copy(last, rest, rest_sem)
    rest_fetch.start()
    for part in range(parts):
        fetch(part).start()
    label = label_of(labels, first, count)
    rest_fetch.wait()

    def add(part, carry):
        onehot = onehot_rows(label, part * 256, (256, count * CHIPS))
        fetch(part).wait()
        width = rest.shape[-1]
        for piece in range(rest.shape[0]):
            x, lanes = piece * width // B, piece * width % B
            lanes = slice(lanes, lanes + width)
            total = jnp.dot(
                onehot, rest[piece], preferred_element_type=jnp.float32
            ).reshape(8, SECTORS, width)
            total = total + held[pl.ds(part * 8, 8), x, :, lanes].astype(jnp.float32)
            held[pl.ds(part * 8, 8), x, :, lanes] = total.astype(jnp.bfloat16)
        store(part).start()
        return carry

    lax.fori_loop(0, parts, add, 0)
    for part in range(parts):
        store(part).wait()


def finished(slots, labels, partial, last):
    count = last_count(slots)
    anywhere = pl.BlockSpec(memory_space=pl.ANY)
    return pl.pallas_call(
        functools.partial(finish_kernel, slots - count, count),
        name=f"finish_{slots}",
        out_shape=jax.ShapeDtypeStruct(partial.shape, partial.dtype),
        in_specs=[pl.BlockSpec(memory_space=pltpu.VMEM), anywhere, anywhere],
        out_specs=anywhere,
        scratch_shapes=[
            pltpu.VMEM(partial.shape, partial.dtype),
            pltpu.VMEM(last.shape, last.dtype),
            pltpu.SemaphoreType.DMA((SECTORS // 8,)),
            pltpu.SemaphoreType.DMA,
        ],
        compiler_params=pltpu.CompilerParams(vmem_limit_bytes=VMEM_LIMIT),
        cost_estimate=pl.CostEstimate(
            flops=2 * SECTORS**2 * count * CHIPS * ROWS * B,
            bytes_accessed=9 * 2**20,
            transcendentals=0,
        ),
    )(labels, partial, last)


def local(psi, env_left, env_right, left_target, right_target, qn_left, qn_right):
    items, sources, labels, choice = tables(left_target, right_target, qn_left, qn_right)

    def branch(depth, slots, operands):
        labels = operands[2]
        return finished(slots, labels, *exchanged(depth, slots, *operands))

    return lax.switch(
        choice[0, 0],
        [functools.partial(branch, depth, slots) for depth, slots in SIZES],
        (items, sources, labels, psi, env_left, env_right),
    )


def solution(mesh):
    fine = Mesh(
        mesh.devices.reshape(CHIPS_Z, CORES, RIGHT), ("z", "core", "right")
    )
    left = ("z", "core")
    return jax.shard_map(
        local,
        mesh=fine,
        in_specs=(
            P(left, None, "right", None),
            P(None, left, None, None),
            P(None, "right", None, None),
            P(),
            P(),
            P(),
            P(),
        ),
        out_specs=P(None, ("z", "core", "right"), None, None),
        check_vma=False,
    )
```

```python
import functools

import jax
import jax.numpy as jnp
from jax import lax
from jax.experimental import pallas as pl
from jax.experimental.pallas import tpu as pltpu
from jax.sharding import Mesh, PartitionSpec as P

filling_charge = 3
B = 512
SECTORS = 32
TERMS = 2
CHIPS_Z = 4
CORES = 2
RIGHT = 16
CHIPS = CHIPS_Z * RIGHT
LEFT_DEV = SECTORS // (CHIPS_Z * CORES)
RIGHT_DEV = SECTORS // RIGHT
ITEMS = TERMS * LEFT_DEV * RIGHT_DEV
HALF = B // CORES
ROWS = B // (CHIPS * CORES)
MESH = pl.DeviceIdType.MESH
VMEM_LIMIT = 60 * 2**20
SIZES = ((10, 12), (10, 14), (12, 16), (12, 18), (16, 32))


def table_kernel(left_target, right_target, qn_left, qn_right, items, sources, labels, most):
    f32, bf16 = jnp.float32, jnp.bfloat16
    square = (SECTORS, SECTORS)
    row = lax.broadcasted_iota(jnp.int32, square, 0)
    column = lax.broadcasted_iota(jnp.int32, square, 1)
    wide = lambda value: value.astype(f32)
    dot = lambda a, b: jnp.dot(a.astype(bf16), b.astype(bf16), preferred_element_type=f32)
    upright = lambda line: jnp.sum(
        jnp.where(row == column, wide(line), 0.0), axis=1, keepdims=True
    )
    charge_left = qn_left[...]
    charge_right = upright(qn_right[...])

    pair = wide(row // RIGHT_DEV == column // RIGHT_DEV)
    second = wide((row + 1 == column) & (column % RIGHT_DEV == 1))
    same = row // LEFT_DEV == column // LEFT_DEV
    core = wide(row // LEFT_DEV % CORES)
    swap = wide(column == row + LEFT_DEV - 2 * LEFT_DEV * (row // LEFT_DEV % CORES))
    active, to_left, to_right, rank, total = [], [], [], [], []
    for t in range(TERMS):
        lefts = upright(left_target[t : t + 1, :])
        rights = wide(right_target[t : t + 1, :])
        hit_left = wide(column) == lefts
        hit_right = wide(row) == rights
        have_left = jnp.sum(jnp.where(hit_left, wide(charge_left), 0.0), axis=1, keepdims=True)
        have_right = jnp.sum(jnp.where(hit_right, charge_right, 0.0), axis=0, keepdims=True)
        allowed = have_left + have_right == float(filling_charge)
        ones = jnp.where(allowed, 1.0, 0.0)
        count = dot(ones, pair)
        active.append(allowed)
        to_left.append(lefts)
        to_right.append(rights)
        rank.append(dot(wide(same & (column < row)), count) + dot(ones, second))
        total.append(dot(wide(same), count))
    rank[1] = rank[1] + total[0]
    own = total[0] + total[1]
    other = dot(swap, own)
    slot = [r + jnp.minimum(other, r + core) for r in rank]

    lane = lax.broadcasted_iota(jnp.int32, (SECTORS, 128), 1)
    tall = lax.broadcasted_iota(jnp.int32, (SECTORS, 128), 0)
    device_lane = tall // RIGHT_DEV == lane % RIGHT
    device_row = tall // LEFT_DEV == lane // RIGHT
    chip_row = tall // (CORES * LEFT_DEV) == lane % CHIPS // RIGHT

    def spread(steps, place, values, rows):
        stack = []
        for k in steps:
            picked = jnp.zeros(square, f32)
            for t in range(TERMS):
                picked = picked + jnp.where(
                    active[t] & (place[t] == float(k)), values[t], 0.0
                )
            stack.append(picked.astype(bf16))
        lanes = dot(jnp.concatenate(stack, axis=0), wide(device_lane))
        lanes = lanes.reshape(len(stack), SECTORS, 128)
        return jnp.sum(jnp.where(rows[None], lanes, 0.0), axis=1)

    item = wide(row % LEFT_DEV * RIGHT_DEV + column % RIGHT_DEV)
    items[...] = spread(
        range(ITEMS), rank, [item, item + float(LEFT_DEV * RIGHT_DEV)], device_row
    ).astype(jnp.int32)

    half_lane = lax.broadcasted_iota(jnp.int32, (ITEMS, 128), 1)

    def by_slot(values):
        both = spread(
            [*range(0, 2 * ITEMS, 2), *range(1, 2 * ITEMS, 2)], slot, values, chip_row
        )
        return jnp.where(half_lane < CHIPS, both[:ITEMS], both[ITEMS:])

    sources[...] = by_slot([core * ITEMS + r for r in rank]).astype(jnp.int32)
    full = jnp.zeros(square, f32)
    high = by_slot([full + lefts + 1.0 for lefts in to_left])
    low = by_slot([full + rights for rights in to_right])
    labels[...] = ((high - 1.0) * SECTORS + low).astype(jnp.int32)
    most_device = jnp.max(own)
    most_chip = jnp.max(own + other)
    choice = jnp.int32(0)
    for depth, slots in SIZES[:-1]:
        choice = choice + jnp.where(
            (most_device > float(depth)) | (most_chip > float(slots)), 1, 0
        )
    most[0, 0] = choice


def tables(left_target, right_target, qn_left, qn_right):
    vmem = pl.BlockSpec(memory_space=pltpu.VMEM)
    table = jax.ShapeDtypeStruct((ITEMS, 128), jnp.int32)
    return pl.pallas_call(
        table_kernel,
        name="tables",
        out_shape=[table, table, table, jax.ShapeDtypeStruct((1, 1), jnp.int32)],
        in_specs=[vmem] * 4,
        out_specs=[vmem] * 3 + [pl.BlockSpec(memory_space=pltpu.SMEM)],
        cost_estimate=pl.CostEstimate(flops=2**24, bytes_accessed=2**15, transcendentals=0),
    )(
        left_target,
        right_target,
        qn_left.reshape(1, SECTORS),
        qn_right.reshape(1, SECTORS),
    )


def fours_of(slots):
    return (slots - 2) // 4


def last_count(slots):
    return 4 if slots % 4 == 2 else 2


def last_shape(count):
    return ROWS * 4 // count, count * CHIPS, B * count // 4


def onehot_rows(label, first, shape):
    row = first + lax.broadcasted_iota(jnp.int32, shape, 0)
    return jnp.where(row == label, 1.0, 0.0).astype(jnp.bfloat16)


def label_of(labels, first, count):
    return jnp.concatenate(
        [labels[pl.ds(first // 2 + p, 1), :] for p in range(count // 2)], axis=1
    )


def exchange(shape_from, shape_to):
    row = lax.broadcasted_iota(jnp.int32, (256, 256), 0)
    column = lax.broadcasted_iota(jnp.int32, (256, 256), 1)
    source = row % shape_from * shape_to + row // shape_from
    return jnp.where(column == source, 1.0, 0.0).astype(jnp.bfloat16)


def reorder(onehot, rows):
    return jnp.dot(onehot, rows, preferred_element_type=jnp.float32).astype(jnp.bfloat16)


def order(incoming, count, sorted_rows):
    unsort = exchange(16, 16)

    def sort(far_z, carry):
        rows = incoming[pl.ds(far_z * RIGHT, RIGHT)]
        rows = reorder(unsort, rows.reshape(256, rows.shape[-1]))
        for piece in range(16):
            start = pl.multiple_of(piece % count * CHIPS + far_z * RIGHT, RIGHT)
            sorted_rows[piece // count, pl.ds(start, RIGHT), :] = rows[
                piece * RIGHT : (piece + 1) * RIGHT
            ]
        return carry

    lax.fori_loop(0, CHIPS_Z, sort, 0, unroll=2)


def exchange_kernel(
    depth,
    slots,
    items,
    sources,
    labels,
    psi_hbm,
    left_hbm,
    right_hbm,
    out,
    last,
    landed,
    psi,
    left,
    right,
    product,
    both,
    send,
    arrived,
    send_pair,
    arrived_pair,
    partial,
    ordered,
    ordered_pair,
    in_sem,
    own_sem,
    pair_send_sem,
    pair_recv_sem,
    free_sem,
    self_sem,
    send_sem,
    recv_sem,
    out_sem,
):
    z = lax.axis_index("z")
    core = lax.axis_index("core")
    place = lax.axis_index("right")
    other = 1 - core
    partner = (z, other, place)
    here = z * RIGHT + place
    device = (z * CORES + core) * RIGHT + place
    fours = fours_of(slots)
    stages = -(-(depth + 2) // 4)
    ends_in_pair = last_count(slots) == 2

    psi_rows = psi_hbm.reshape(LEFT_DEV, B * RIGHT_DEV, B)
    psi_load = [
        pltpu.make_async_copy(psi_rows.at[a], landed.at[a], in_sem.at[a])
        for a in range(LEFT_DEV)
    ]
    left_load = pltpu.make_async_copy(left_hbm, left, in_sem.at[LEFT_DEV])
    right_load = pltpu.make_async_copy(right_hbm, right, in_sem.at[LEFT_DEV + 1])
    for load in psi_load:
        load.start()

    steps = (1, 3, 2, 0)
    way = 1 - 2 * core
    route = []
    for i in range(RIGHT):
        step_x = steps[i % 4]
        step_y = steps[(i + i // 4) % 4]
        far_x = (place // 4 + 4 + way * step_x) % 4
        far_y = (place % 4 + 4 + way * step_y) % 4
        route.append((step_x + step_y, steps[(i + i // 4 * 2) % 4], far_x * 4 + far_y))

    def for_others(visit):
        def turn(shift, carry):
            far_z = [
                (z + 2 * CHIPS_Z + way * (shift + step)) % CHIPS_Z for step in range(CHIPS_Z)
            ]
            for moved, step, far_place in route:
                if moved or step:
                    visit(far_z[step], far_place)
                else:
                    pl.when(shift > 0)(functools.partial(visit, far_z[step], far_place))
            return carry

        lax.fori_loop(0, CHIPS_Z, turn, 0)

    barrier = pltpu.get_barrier_semaphore()
    pl.semaphore_signal(barrier, inc=1, device_id=partner, device_id_type=MESH)

    def greet(far_z, far_place):
        pl.semaphore_signal(
            barrier, inc=1, device_id=(far_z, core, far_place), device_id_type=MESH
        )

    for_others(greet)

    unmix = exchange(128, RIGHT_DEV)

    def split(a, carry):
        for part in range(B // 128):
            apart = reorder(unmix, landed[a, part * 256 : part * 256 + 256, :])
            for b in range(RIGHT_DEV):
                psi[a * RIGHT_DEV + b, part * 128 : part * 128 + 128, :] = apart[
                    b * 128 : (b + 1) * 128
                ]
        return carry

    psi_load[0].wait()
    left_load.start()
    right_load.start()
    split(0, 0)

    def next_split(a, carry):
        pltpu.make_async_copy(psi_rows.at[a], landed.at[a], in_sem.at[a]).wait()
        return split(a, carry)

    lax.fori_loop(1, LEFT_DEV, next_split, 0)
    left_load.wait()
    right_load.wait()

    def own_copy(rank):
        return pltpu.make_async_copy(
            product.at[rank, :, core], both.at[core * depth + rank], own_sem.at[rank]
        )

    def pair_copy(rank):
        return pltpu.make_async_remote_copy(
            src_ref=product.at[rank, :, other],
            dst_ref=both.at[core * depth + rank],
            send_sem=pair_send_sem.at[rank],
            recv_sem=pair_recv_sem.at[rank],
            device_id=partner,
            device_id_type=MESH,
        )

    def multiply_two(step, carry):
        ranks = (2 * step, 2 * step + 1)
        halves, rights = [], []
        for rank in ranks:
            item = items[rank, device]
            term = item // (LEFT_DEV * RIGHT_DEV)
            pair = item % (LEFT_DEV * RIGHT_DEV)
            half = jnp.dot(
                left[term * LEFT_DEV + pair // RIGHT_DEV],
                psi[pair],
                preferred_element_type=jnp.float32,
            )
            halves.append(half.astype(jnp.bfloat16))
            rights.append(right[term * RIGHT_DEV + pair % RIGHT_DEV])
        for rank, half, by in zip(ranks, halves, rights):
            moved = lax.dot_general(
                half, by, (((1,), (1,)), ((), ())), preferred_element_type=jnp.float32
            ).astype(jnp.bfloat16)
            product[rank] = moved.reshape(CHIPS_Z, CORES, B // (CHIPS_Z * CORES), B)

        @pl.when(step == 0)
        def _():
            pl.semaphore_wait(barrier, CHIPS)

        @pl.when((step > 0) & (step % 2 == 1))
        def _():
            pl.semaphore_wait(free_sem, 1)

        for rank in ranks:
            pair_copy(rank).start()
            own_copy(rank).start()
        return carry

    def arrive(rank, carry):
        own_copy(rank).wait()
        pair_copy(rank).wait_recv()
        return carry

    def departing(outgoing, incoming, chunk, far_z, far_place):
        pltpu.make_async_remote_copy(
            src_ref=outgoing.at[far_z * RIGHT + far_place],
            dst_ref=incoming.at[here],
            send_sem=send_sem.at[chunk],
            recv_sem=recv_sem.at[chunk],
            device_id=(far_z, core, far_place),
            device_id_type=MESH,
        ).start()

    def self_copy(outgoing, incoming, chunk):
        return pltpu.make_async_copy(
            outgoing.at[here], incoming.at[here], self_sem.at[chunk]
        )

    mix = exchange(4, 64)

    def pack(outgoing, first, count):
        def quarter(far_z, carry):
            def block(k):
                source = sources[first // 2 + k // 2, k % 2 * CHIPS + here]
                return both[source // ITEMS * depth + source % ITEMS, far_z]

            blocks = [block(k) for k in range(count)]
            if count == 2:
                blocks = [rows[:, : B // 2] for rows in blocks] + [rows[:, B // 2 :] for rows in blocks]
            rows = reorder(mix, jnp.concatenate(blocks, axis=0))
            outgoing[pl.ds(far_z * RIGHT, RIGHT)] = rows.reshape(
                RIGHT, 4 * ROWS, rows.shape[-1]
            )
            return carry

        lax.fori_loop(0, CHIPS_Z, quarter, 0, unroll=2)

    def packed(outgoing, incoming, chunk, first, count):
        pack(outgoing, first, count)
        self_copy(outgoing, incoming, chunk).start()
        for_others(functools.partial(departing, outgoing, incoming, chunk))

    def stage(turn, carry):
        start = jnp.maximum(4 * turn - 2, 0)
        stop = jnp.maximum(jnp.minimum(4 * turn + 2, depth), start)
        lax.fori_loop(start // 2, stop // 2, multiply_two, 0)
        lax.fori_loop(start, stop, arrive, 0)

        @pl.when(turn == 0)
        def _():
            packed(send_pair.at[0], arrived_pair.at[0], fours, 0, 2)

        @pl.when(turn > 0)
        def _():
            four = turn - 1
            packed(send.at[four], arrived.at[four], four, 2 + 4 * four, 4)

        @pl.when(turn < stages - 1)
        def _():
            pl.semaphore_signal(free_sem, inc=1, device_id=partner, device_id_type=MESH)

        return carry

    lax.fori_loop(0, fours + 1, stage, 0)
    if ends_in_pair:
        packed(send_pair.at[1], arrived_pair.at[1], fours + 1, slots - 2, 2)

    def receive(outgoing, incoming, chunk):
        self_copy(outgoing, incoming, chunk).wait()
        arrivals = incoming.at[pl.ds(0, CHIPS - 1)]
        pltpu.make_async_copy(arrivals, arrivals, recv_sem.at[chunk]).wait()

    partial[...] = jnp.zeros(partial.shape, partial.dtype)

    def place_chunk(first, count, sorted_rows):
        label = label_of(labels, first, count)
        pieces, _, width = sorted_rows.shape

        def put(part, carry):
            onehot = onehot_rows(label, part * 256, (256, count * CHIPS))

            def row(x, carry):
                for half in range(pieces // ROWS):
                    lanes = slice(half * width, half * width + width)
                    total = jnp.dot(
                        onehot,
                        sorted_rows[x * (pieces // ROWS) + half],
                        preferred_element_type=jnp.float32,
                    ).reshape(8, SECTORS, width)
                    total = total + partial[pl.ds(part * 8, 8), x, :, lanes].astype(jnp.float32)
                    partial[pl.ds(part * 8, 8), x, :, lanes] = total.astype(jnp.bfloat16)
                return carry

            return lax.fori_loop(0, ROWS, row, carry, unroll=2)

        lax.fori_loop(0, SECTORS // 8, put, 0)

    receive(send_pair.at[0], arrived_pair.at[0], fours)
    order(arrived_pair.at[0], 2, ordered_pair)
    place_chunk(0, 2, ordered_pair)
    placed = fours if ends_in_pair else fours - 1

    def collect(four, carry):
        receive(send.at[four], arrived.at[four], four)

        @pl.when(four < placed)
        def _():
            order(arrived.at[four], 4, ordered)
            place_chunk(2 + 4 * four, 4, ordered)

        @pl.when(four == placed - 1)
        def _():
            pltpu.make_async_copy(partial, out, out_sem.at[0]).start()

        return carry

    lax.fori_loop(0, fours, collect, 0)
    rest = arrived.at[fours - 1]
    if ends_in_pair:
        receive(send_pair.at[1], arrived_pair.at[1], fours + 1)
        rest = arrived_pair.at[1]
    rest_out = pltpu.make_async_copy(rest, last, out_sem.at[1])
    rest_out.start()

    def sent(rank, carry):
        pair_copy(rank).wait_send()
        return carry

    lax.fori_loop(0, depth, sent, 0)

    def gone(chunk, carry):
        departures = send.at[chunk, pl.ds(0, CHIPS - 1)]
        pltpu.make_async_copy(departures, departures, send_sem.at[chunk]).wait()
        return carry

    lax.fori_loop(0, fours, gone, 0)
    for pair in range(1 + ends_in_pair):
        departures = send_pair.at[pair, pl.ds(0, CHIPS - 1)]
        pltpu.make_async_copy(departures, departures, send_sem.at[fours + pair]).wait()
    pltpu.make_async_copy(partial, out, out_sem.at[0]).wait()
    rest_out.wait()


def exchanged(depth, slots, items, sources, labels, psi, env_left, env_right):
    smem = pl.BlockSpec(memory_space=pltpu.SMEM)
    anywhere = pl.BlockSpec(memory_space=pl.ANY)
    vmem = pl.BlockSpec(memory_space=pltpu.VMEM)
    bf16 = jnp.bfloat16
    fours = fours_of(slots)
    messages = (CHIPS, 4 * ROWS, B)
    pair_messages = (2, CHIPS, 4 * ROWS, B // 2)
    dma = pltpu.SemaphoreType.DMA
    return pl.pallas_call(
        functools.partial(exchange_kernel, depth, slots),
        name=f"exchange_{slots}",
        out_shape=[
            jax.ShapeDtypeStruct((SECTORS, ROWS, SECTORS, B), bf16),
            jax.ShapeDtypeStruct((CHIPS, 4 * ROWS, B * last_count(slots) // 4), bf16),
        ],
        in_specs=[smem] * 2 + [vmem] + [anywhere] * 3,
        out_specs=[anywhere] * 2,
        scratch_shapes=[
            pltpu.VMEM((LEFT_DEV, B * RIGHT_DEV, B), bf16),
            pltpu.VMEM((LEFT_DEV * RIGHT_DEV, B, B), bf16),
            pltpu.VMEM((TERMS * LEFT_DEV, B, B), bf16),
            pltpu.VMEM((TERMS * RIGHT_DEV, B, B), bf16),
            pltpu.VMEM((depth, CHIPS_Z, CORES, B // (CHIPS_Z * CORES), B), bf16),
            pltpu.VMEM((CORES * depth, CHIPS_Z, B // (CHIPS_Z * CORES), B), bf16),
            pltpu.VMEM((fours, *messages), bf16),
            pltpu.VMEM((fours, *messages), bf16),
            pltpu.VMEM(pair_messages, bf16),
            pltpu.VMEM(pair_messages, bf16),
            pltpu.VMEM((SECTORS, ROWS, SECTORS, B), bf16),
            pltpu.VMEM(last_shape(4), bf16),
            pltpu.VMEM(last_shape(2), bf16),
            dma((LEFT_DEV + 2,)),
            dma((depth,)),
            dma((depth,)),
            dma((depth,)),
            pltpu.SemaphoreType.REGULAR,
            dma((fours + 2,)),
            dma((fours + 2,)),
            dma((fours + 2,)),
            dma((2,)),
        ],
        compiler_params=pltpu.CompilerParams(
            collective_id=slots // 2,
            has_side_effects=True,
            vmem_limit_bytes=VMEM_LIMIT,
        ),
        cost_estimate=pl.CostEstimate(
            flops=4 * depth * B**3, bytes_accessed=14 * 2**20, transcendentals=0
        ),
    )(
        items,
        sources,
        labels,
        psi,
        env_left.reshape(TERMS * LEFT_DEV, B, B),
        env_right.reshape(TERMS * RIGHT_DEV, B, B),
    )


def finish_kernel(
    first, count, labels, partial, last, out, held, arrived, rest, sem, rest_sem
):
    step = 4
    parts = SECTORS // step

    def fetch(part):
        rows = pl.ds(part * step, step)
        return pltpu.make_async_copy(partial.at[rows], held.at[rows], sem.at[part])

    def store(part):
        rows = pl.ds(part * step, step)
        return pltpu.make_async_copy(held.at[rows], out.at[rows], sem.at[part])

    rest_fetch = pltpu.make_async_copy(last, arrived, rest_sem)
    rest_fetch.start()
    for part in range(parts):
        fetch(part).start()
    label = label_of(labels, first, count)
    rest_fetch.wait()
    order(arrived, count, rest)

    def add(part, carry):
        onehot = onehot_rows(label, part * step * SECTORS, (step * SECTORS, count * CHIPS))
        fetch(part).wait()
        width = rest.shape[-1]
        here = pl.ds(part * step, step)
        for piece in range(rest.shape[0]):
            x, lanes = piece * width // B, piece * width % B
            lanes = slice(lanes, lanes + width)
            total = jnp.dot(
                onehot, rest[piece], preferred_element_type=jnp.float32
            ).reshape(step, SECTORS, width)
            total = total + held[here, x, :, lanes].astype(jnp.float32)
            held[here, x, :, lanes] = total.astype(jnp.bfloat16)
        store(part).start()
        return carry

    lax.fori_loop(0, parts, add, 0)
    for part in range(parts):
        store(part).wait()


def finished(slots, labels, partial, last):
    count = last_count(slots)
    anywhere = pl.BlockSpec(memory_space=pl.ANY)
    return pl.pallas_call(
        functools.partial(finish_kernel, slots - count, count),
        name=f"finish_{slots}",
        out_shape=jax.ShapeDtypeStruct(partial.shape, partial.dtype),
        in_specs=[pl.BlockSpec(memory_space=pltpu.VMEM), anywhere, anywhere],
        out_specs=anywhere,
        scratch_shapes=[
            pltpu.VMEM(partial.shape, partial.dtype),
            pltpu.VMEM(last.shape, last.dtype),
            pltpu.VMEM(last_shape(count), last.dtype),
            pltpu.SemaphoreType.DMA((SECTORS // 4,)),
            pltpu.SemaphoreType.DMA,
        ],
        compiler_params=pltpu.CompilerParams(vmem_limit_bytes=VMEM_LIMIT),
        cost_estimate=pl.CostEstimate(
            flops=2 * SECTORS**2 * count * CHIPS * ROWS * B,
            bytes_accessed=9 * 2**20,
            transcendentals=0,
        ),
    )(labels, partial, last)


def local(psi, env_left, env_right, left_target, right_target, qn_left, qn_right):
    items, sources, labels, choice = tables(left_target, right_target, qn_left, qn_right)

    def branch(depth, slots, operands):
        labels = operands[2]
        return finished(slots, labels, *exchanged(depth, slots, *operands))

    return lax.switch(
        choice[0, 0],
        [functools.partial(branch, depth, slots) for depth, slots in SIZES],
        (items, sources, labels, psi, env_left, env_right),
    )


def solution(mesh):
    fine = Mesh(
        mesh.devices.reshape(CHIPS_Z, CORES, RIGHT), ("z", "core", "right")
    )
    left = ("z", "core")
    return jax.shard_map(
        local,
        mesh=fine,
        in_specs=(
            P(left, None, "right", None),
            P(None, left, None, None),
            P(None, "right", None, None),
            P(),
            P(),
            P(),
            P(),
        ),
        out_specs=P(None, ("z", "core", "right"), None, None),
        check_vma=False,
    )
```

```python
import functools

import jax
import jax.numpy as jnp
from jax import lax
from jax.experimental import pallas as pl
from jax.experimental.pallas import tpu as pltpu
from jax.sharding import Mesh, PartitionSpec as P

filling_charge = 3
B = 512
SECTORS = 32
TERMS = 2
CHIPS_Z = 4
CORES = 2
RIGHT = 16
CHIPS = CHIPS_Z * RIGHT
LEFT_DEV = SECTORS // (CHIPS_Z * CORES)
RIGHT_DEV = SECTORS // RIGHT
ITEMS = TERMS * LEFT_DEV * RIGHT_DEV
HALF = B // CORES
ROWS = B // (CHIPS * CORES)
MESH = pl.DeviceIdType.MESH
VMEM_LIMIT = 60 * 2**20
SIZES = ((10, 12), (10, 14), (12, 16), (12, 18), (16, 32))


def table_kernel(left_target, right_target, qn_left, qn_right, items, sources, labels, most):
    f32, bf16 = jnp.float32, jnp.bfloat16
    square = (SECTORS, SECTORS)
    row = lax.broadcasted_iota(jnp.int32, square, 0)
    column = lax.broadcasted_iota(jnp.int32, square, 1)
    wide = lambda value: value.astype(f32)
    dot = lambda a, b: jnp.dot(a.astype(bf16), b.astype(bf16), preferred_element_type=f32)
    upright = lambda line: jnp.sum(
        jnp.where(row == column, wide(line), 0.0), axis=1, keepdims=True
    )
    charge_left = qn_left[...]
    charge_right = upright(qn_right[...])

    pair = wide(row // RIGHT_DEV == column // RIGHT_DEV)
    second = wide((row + 1 == column) & (column % RIGHT_DEV == 1))
    same = row // LEFT_DEV == column // LEFT_DEV
    core = wide(row // LEFT_DEV % CORES)
    swap = wide(column == row + LEFT_DEV - 2 * LEFT_DEV * (row // LEFT_DEV % CORES))
    active, to_left, to_right, rank, total = [], [], [], [], []
    for t in range(TERMS):
        lefts = upright(left_target[t : t + 1, :])
        rights = wide(right_target[t : t + 1, :])
        hit_left = wide(column) == lefts
        hit_right = wide(row) == rights
        have_left = jnp.sum(jnp.where(hit_left, wide(charge_left), 0.0), axis=1, keepdims=True)
        have_right = jnp.sum(jnp.where(hit_right, charge_right, 0.0), axis=0, keepdims=True)
        allowed = have_left + have_right == float(filling_charge)
        ones = jnp.where(allowed, 1.0, 0.0)
        count = dot(ones, pair)
        active.append(allowed)
        to_left.append(lefts)
        to_right.append(rights)
        rank.append(dot(wide(same & (column < row)), count) + dot(ones, second))
        total.append(dot(wide(same), count))
    rank[1] = rank[1] + total[0]
    own = total[0] + total[1]
    other = dot(swap, own)
    slot = [r + jnp.minimum(other, r + core) for r in rank]

    lane = lax.broadcasted_iota(jnp.int32, (SECTORS, 128), 1)
    tall = lax.broadcasted_iota(jnp.int32, (SECTORS, 128), 0)
    device_lane = tall // RIGHT_DEV == lane % RIGHT
    device_row = tall // LEFT_DEV == lane // RIGHT
    chip_row = tall // (CORES * LEFT_DEV) == lane % CHIPS // RIGHT

    def spread(steps, place, values, rows):
        stack = []
        for k in steps:
            picked = jnp.zeros(square, f32)
            for t in range(TERMS):
                picked = picked + jnp.where(
                    active[t] & (place[t] == float(k)), values[t], 0.0
                )
            stack.append(picked.astype(bf16))
        lanes = dot(jnp.concatenate(stack, axis=0), wide(device_lane))
        lanes = lanes.reshape(len(stack), SECTORS, 128)
        return jnp.sum(jnp.where(rows[None], lanes, 0.0), axis=1)

    item = wide(row % LEFT_DEV * RIGHT_DEV + column % RIGHT_DEV)
    items[...] = spread(
        range(ITEMS), rank, [item, item + float(LEFT_DEV * RIGHT_DEV)], device_row
    ).astype(jnp.int32)

    half_lane = lax.broadcasted_iota(jnp.int32, (ITEMS, 128), 1)

    def by_slot(values):
        both = spread(
            [*range(0, 2 * ITEMS, 2), *range(1, 2 * ITEMS, 2)], slot, values, chip_row
        )
        return jnp.where(half_lane < CHIPS, both[:ITEMS], both[ITEMS:])

    sources[...] = by_slot([core * ITEMS + r for r in rank]).astype(jnp.int32)
    full = jnp.zeros(square, f32)
    high = by_slot([full + lefts + 1.0 for lefts in to_left])
    low = by_slot([full + rights for rights in to_right])
    labels[...] = ((high - 1.0) * SECTORS + low).astype(jnp.int32)
    most_device = jnp.max(own)
    most_chip = jnp.max(own + other)
    choice = jnp.int32(0)
    for depth, slots in SIZES[:-1]:
        choice = choice + jnp.where(
            (most_device > float(depth)) | (most_chip > float(slots)), 1, 0
        )
    most[0, 0] = choice


def tables(left_target, right_target, qn_left, qn_right):
    vmem = pl.BlockSpec(memory_space=pltpu.VMEM)
    table = jax.ShapeDtypeStruct((ITEMS, 128), jnp.int32)
    return pl.pallas_call(
        table_kernel,
        name="tables",
        out_shape=[table, table, table, jax.ShapeDtypeStruct((1, 1), jnp.int32)],
        in_specs=[vmem] * 4,
        out_specs=[vmem] * 3 + [pl.BlockSpec(memory_space=pltpu.SMEM)],
        cost_estimate=pl.CostEstimate(flops=2**24, bytes_accessed=2**15, transcendentals=0),
    )(
        left_target,
        right_target,
        qn_left.reshape(1, SECTORS),
        qn_right.reshape(1, SECTORS),
    )


def fours_of(slots):
    return (slots - 2) // 4


def last_count(slots):
    return 4 if slots % 4 == 2 else 2


def last_shape(count):
    return ROWS * 4 // count, count * CHIPS, B * count // 4


def onehot_rows(label, first, shape):
    row = first + lax.broadcasted_iota(jnp.int32, shape, 0)
    return jnp.where(row == label, 1.0, 0.0).astype(jnp.bfloat16)


def label_of(labels, first, count):
    return jnp.concatenate(
        [labels[pl.ds(first // 2 + p, 1), :] for p in range(count // 2)], axis=1
    )


def exchange(shape_from, shape_to):
    row = lax.broadcasted_iota(jnp.int32, (256, 256), 0)
    column = lax.broadcasted_iota(jnp.int32, (256, 256), 1)
    source = row % shape_from * shape_to + row // shape_from
    return jnp.where(column == source, 1.0, 0.0).astype(jnp.bfloat16)


def reorder(onehot, rows):
    return jnp.dot(onehot, rows, preferred_element_type=jnp.float32).astype(jnp.bfloat16)


def order(incoming, count, sorted_rows):
    unsort = exchange(16, 16)

    def sort(far_z, carry):
        rows = incoming[pl.ds(far_z * RIGHT, RIGHT)]
        rows = reorder(unsort, rows.reshape(256, rows.shape[-1]))
        for piece in range(16):
            start = pl.multiple_of(piece % count * CHIPS + far_z * RIGHT, RIGHT)
            sorted_rows[piece // count, pl.ds(start, RIGHT), :] = rows[
                piece * RIGHT : (piece + 1) * RIGHT
            ]
        return carry

    lax.fori_loop(0, CHIPS_Z, sort, 0, unroll=2)


def exchange_kernel(
    depth,
    slots,
    items,
    sources,
    labels,
    psi_hbm,
    left_hbm,
    right_hbm,
    out,
    last,
    landed,
    psi,
    left,
    right,
    product,
    both,
    send,
    arrived,
    send_pair,
    arrived_pair,
    partial,
    ordered,
    ordered_pair,
    in_sem,
    own_sem,
    pair_send_sem,
    pair_recv_sem,
    free_sem,
    self_sem,
    send_sem,
    recv_sem,
    out_sem,
):
    z = lax.axis_index("z")
    core = lax.axis_index("core")
    place = lax.axis_index("right")
    other = 1 - core
    partner = (z, other, place)
    here = z * RIGHT + place
    device = (z * CORES + core) * RIGHT + place
    fours = fours_of(slots)
    stages = -(-(depth + 2) // 4)
    ends_in_pair = last_count(slots) == 2

    psi_rows = psi_hbm.reshape(LEFT_DEV, B * RIGHT_DEV, B)
    psi_load = [
        pltpu.make_async_copy(psi_rows.at[a], landed.at[a], in_sem.at[a])
        for a in range(LEFT_DEV)
    ]
    left_load = pltpu.make_async_copy(left_hbm, left, in_sem.at[LEFT_DEV])
    right_load = pltpu.make_async_copy(right_hbm, right, in_sem.at[LEFT_DEV + 1])
    for load in psi_load:
        load.start()

    steps = (1, 3, 2, 0)
    way = 1 - 2 * core
    route = []
    for i in range(RIGHT):
        step_x = steps[i % 4]
        step_y = steps[(i + i // 4) % 4]
        far_x = (place // 4 + 4 + way * step_x) % 4
        far_y = (place % 4 + 4 + way * step_y) % 4
        route.append((step_x + step_y, steps[(i + i // 4 * 2) % 4], far_x * 4 + far_y))

    def for_others(visit):
        def turn(shift, carry):
            far_z = [
                (z + 2 * CHIPS_Z + way * (shift + step)) % CHIPS_Z for step in range(CHIPS_Z)
            ]
            for moved, step, far_place in route:
                if moved or step:
                    visit(far_z[step], far_place)
                else:
                    pl.when(shift > 0)(functools.partial(visit, far_z[step], far_place))
            return carry

        lax.fori_loop(0, CHIPS_Z, turn, 0)

    barrier = pltpu.get_barrier_semaphore()
    pl.semaphore_signal(barrier, inc=1, device_id=partner, device_id_type=MESH)

    def greet(far_z, far_place):
        pl.semaphore_signal(
            barrier, inc=1, device_id=(far_z, core, far_place), device_id_type=MESH
        )

    for_others(greet)

    unmix = exchange(128, RIGHT_DEV)

    def split(a, carry):
        for part in range(B // 128):
            apart = reorder(unmix, landed[a, part * 256 : part * 256 + 256, :])
            for b in range(RIGHT_DEV):
                psi[a * RIGHT_DEV + b, part * 128 : part * 128 + 128, :] = apart[
                    b * 128 : (b + 1) * 128
                ]
        return carry

    psi_load[0].wait()
    left_load.start()
    right_load.start()
    split(0, 0)

    def next_split(a, carry):
        pltpu.make_async_copy(psi_rows.at[a], landed.at[a], in_sem.at[a]).wait()
        return split(a, carry)

    lax.fori_loop(1, LEFT_DEV, next_split, 0)
    left_load.wait()
    right_load.wait()

    def own_copy(rank):
        return pltpu.make_async_copy(
            product.at[rank, :, core], both.at[core * depth + rank], own_sem.at[rank]
        )

    def pair_copy(rank):
        return pltpu.make_async_remote_copy(
            src_ref=product.at[rank, :, other],
            dst_ref=both.at[core * depth + rank],
            send_sem=pair_send_sem.at[rank],
            recv_sem=pair_recv_sem.at[rank],
            device_id=partner,
            device_id_type=MESH,
        )

    def multiply_two(step):
        ranks = (2 * step, 2 * step + 1)
        halves, rights = [], []
        for rank in ranks:
            item = items[rank, device]
            term = item // (LEFT_DEV * RIGHT_DEV)
            pair = item % (LEFT_DEV * RIGHT_DEV)
            half = jnp.dot(
                left[term * LEFT_DEV + pair // RIGHT_DEV],
                psi[pair],
                preferred_element_type=jnp.float32,
            )
            halves.append(half.astype(jnp.bfloat16))
            rights.append(right[term * RIGHT_DEV + pair % RIGHT_DEV])
        for rank, half, by in zip(ranks, halves, rights):
            moved = lax.dot_general(
                half, by, (((1,), (1,)), ((), ())), preferred_element_type=jnp.float32
            ).astype(jnp.bfloat16)
            product[rank] = moved.reshape(CHIPS_Z, CORES, B // (CHIPS_Z * CORES), B)

    def swap_two(step):
        @pl.when(step == 0)
        def _():
            pl.semaphore_wait(barrier, CHIPS)

        @pl.when((step > 0) & (step % 2 == 1))
        def _():
            pl.semaphore_wait(free_sem, 1)

        for rank in (2 * step, 2 * step + 1):
            pair_copy(rank).start()
            own_copy(rank).start()

    def advance(step, carry):
        pl.when(step >= 0)(lambda: swap_two(step))
        pl.when(step + 1 < depth // 2)(lambda: multiply_two(step + 1))
        return carry

    def arrive(rank, carry):
        own_copy(rank).wait()
        pair_copy(rank).wait_recv()
        return carry

    def departing(outgoing, incoming, chunk, far_z, far_place):
        pltpu.make_async_remote_copy(
            src_ref=outgoing.at[far_z * RIGHT + far_place],
            dst_ref=incoming.at[here],
            send_sem=send_sem.at[chunk],
            recv_sem=recv_sem.at[chunk],
            device_id=(far_z, core, far_place),
            device_id_type=MESH,
        ).start()

    def self_copy(outgoing, incoming, chunk):
        return pltpu.make_async_copy(
            outgoing.at[here], incoming.at[here], self_sem.at[chunk]
        )

    mix = exchange(4, 64)

    def pack(outgoing, first, count):
        def quarter(far_z, carry):
            def block(k):
                source = sources[first // 2 + k // 2, k % 2 * CHIPS + here]
                return both[source // ITEMS * depth + source % ITEMS, far_z]

            blocks = [block(k) for k in range(count)]
            if count == 2:
                blocks = [rows[:, : B // 2] for rows in blocks] + [rows[:, B // 2 :] for rows in blocks]
            rows = reorder(mix, jnp.concatenate(blocks, axis=0))
            outgoing[pl.ds(far_z * RIGHT, RIGHT)] = rows.reshape(
                RIGHT, 4 * ROWS, rows.shape[-1]
            )
            return carry

        lax.fori_loop(0, CHIPS_Z, quarter, 0, unroll=2)

    def depart(outgoing, incoming, chunk):
        self_copy(outgoing, incoming, chunk).start()
        for_others(functools.partial(departing, outgoing, incoming, chunk))

    def stage(turn, carry):
        start = jnp.maximum(4 * turn - 2, 0)
        stop = jnp.maximum(jnp.minimum(4 * turn + 2, depth), start)
        lax.fori_loop(jnp.where(turn == 0, -1, start // 2), stop // 2, advance, 0)
        lax.fori_loop(start, stop, arrive, 0)

        four = jnp.maximum(turn - 1, 0)
        pl.when(turn == 0)(lambda: pack(send_pair.at[0], 0, 2))
        pl.when(turn > 0)(lambda: pack(send.at[four], 2 + 4 * four, 4))

        @pl.when(turn < stages - 1)
        def _():
            pl.semaphore_signal(free_sem, inc=1, device_id=partner, device_id_type=MESH)

        pl.when(turn == 0)(lambda: depart(send_pair.at[0], arrived_pair.at[0], fours))
        pl.when(turn > 0)(lambda: depart(send.at[four], arrived.at[four], four))
        return carry

    lax.fori_loop(0, fours + 1, stage, 0)
    if ends_in_pair:
        pack(send_pair.at[1], slots - 2, 2)
        depart(send_pair.at[1], arrived_pair.at[1], fours + 1)

    def receive(outgoing, incoming, chunk):
        self_copy(outgoing, incoming, chunk).wait()
        arrivals = incoming.at[pl.ds(0, CHIPS - 1)]
        pltpu.make_async_copy(arrivals, arrivals, recv_sem.at[chunk]).wait()

    partial[...] = jnp.zeros(partial.shape, partial.dtype)

    def place_chunk(first, count, sorted_rows):
        label = label_of(labels, first, count)
        pieces, _, width = sorted_rows.shape

        def put(part, carry):
            onehot = onehot_rows(label, part * 256, (256, count * CHIPS))

            def row(x, carry):
                for half in range(pieces // ROWS):
                    lanes = slice(half * width, half * width + width)
                    total = jnp.dot(
                        onehot,
                        sorted_rows[x * (pieces // ROWS) + half],
                        preferred_element_type=jnp.float32,
                    ).reshape(8, SECTORS, width)
                    total = total + partial[pl.ds(part * 8, 8), x, :, lanes].astype(jnp.float32)
                    partial[pl.ds(part * 8, 8), x, :, lanes] = total.astype(jnp.bfloat16)
                return carry

            return lax.fori_loop(0, ROWS, row, carry, unroll=2)

        lax.fori_loop(0, SECTORS // 8, put, 0)

    receive(send_pair.at[0], arrived_pair.at[0], fours)
    order(arrived_pair.at[0], 2, ordered_pair)
    place_chunk(0, 2, ordered_pair)
    placed = fours if ends_in_pair else fours - 1

    def collect(four, carry):
        receive(send.at[four], arrived.at[four], four)
        order(arrived.at[four], 4, ordered)

        @pl.when(four < placed)
        def _():
            place_chunk(2 + 4 * four, 4, ordered)

        @pl.when(four == placed - 1)
        def _():
            pltpu.make_async_copy(partial, out, out_sem.at[0]).start()

        return carry

    lax.fori_loop(0, fours, collect, 0)
    rest = ordered
    if ends_in_pair:
        receive(send_pair.at[1], arrived_pair.at[1], fours + 1)
        order(arrived_pair.at[1], 2, ordered_pair)
        rest = ordered_pair
    rest_out = pltpu.make_async_copy(rest, last, out_sem.at[1])
    rest_out.start()

    def sent(rank, carry):
        pair_copy(rank).wait_send()
        return carry

    lax.fori_loop(0, depth, sent, 0)

    def gone(chunk, carry):
        departures = send.at[chunk, pl.ds(0, CHIPS - 1)]
        pltpu.make_async_copy(departures, departures, send_sem.at[chunk]).wait()
        return carry

    lax.fori_loop(0, fours, gone, 0)
    for pair in range(1 + ends_in_pair):
        departures = send_pair.at[pair, pl.ds(0, CHIPS - 1)]
        pltpu.make_async_copy(departures, departures, send_sem.at[fours + pair]).wait()
    pltpu.make_async_copy(partial, out, out_sem.at[0]).wait()
    rest_out.wait()


def exchanged(depth, slots, items, sources, labels, psi, env_left, env_right):
    smem = pl.BlockSpec(memory_space=pltpu.SMEM)
    anywhere = pl.BlockSpec(memory_space=pl.ANY)
    vmem = pl.BlockSpec(memory_space=pltpu.VMEM)
    bf16 = jnp.bfloat16
    fours = fours_of(slots)
    messages = (CHIPS, 4 * ROWS, B)
    pair_messages = (2, CHIPS, 4 * ROWS, B // 2)
    dma = pltpu.SemaphoreType.DMA
    return pl.pallas_call(
        functools.partial(exchange_kernel, depth, slots),
        name=f"exchange_{slots}",
        out_shape=[
            jax.ShapeDtypeStruct((SECTORS, ROWS, SECTORS, B), bf16),
            jax.ShapeDtypeStruct(last_shape(last_count(slots)), bf16),
        ],
        in_specs=[smem] * 2 + [vmem] + [anywhere] * 3,
        out_specs=[anywhere] * 2,
        scratch_shapes=[
            pltpu.VMEM((LEFT_DEV, B * RIGHT_DEV, B), bf16),
            pltpu.VMEM((LEFT_DEV * RIGHT_DEV, B, B), bf16),
            pltpu.VMEM((TERMS * LEFT_DEV, B, B), bf16),
            pltpu.VMEM((TERMS * RIGHT_DEV, B, B), bf16),
            pltpu.VMEM((depth, CHIPS_Z, CORES, B // (CHIPS_Z * CORES), B), bf16),
            pltpu.VMEM((CORES * depth, CHIPS_Z, B // (CHIPS_Z * CORES), B), bf16),
            pltpu.VMEM((fours, *messages), bf16),
            pltpu.VMEM((fours, *messages), bf16),
            pltpu.VMEM(pair_messages, bf16),
            pltpu.VMEM(pair_messages, bf16),
            pltpu.VMEM((SECTORS, ROWS, SECTORS, B), bf16),
            pltpu.VMEM(last_shape(4), bf16),
            pltpu.VMEM(last_shape(2), bf16),
            dma((LEFT_DEV + 2,)),
            dma((depth,)),
            dma((depth,)),
            dma((depth,)),
            pltpu.SemaphoreType.REGULAR,
            dma((fours + 2,)),
            dma((fours + 2,)),
            dma((fours + 2,)),
            dma((2,)),
        ],
        compiler_params=pltpu.CompilerParams(
            collective_id=slots // 2,
            has_side_effects=True,
            vmem_limit_bytes=VMEM_LIMIT,
        ),
        cost_estimate=pl.CostEstimate(
            flops=4 * depth * B**3, bytes_accessed=14 * 2**20, transcendentals=0
        ),
    )(
        items,
        sources,
        labels,
        psi,
        env_left.reshape(TERMS * LEFT_DEV, B, B),
        env_right.reshape(TERMS * RIGHT_DEV, B, B),
    )


def finish_kernel(first, count, labels, partial, last, out, held, rest, sem, rest_sem):
    parts = held.shape[0] // 8

    def fetch(part):
        rows = pl.ds(part * 8, 8)
        return pltpu.make_async_copy(partial.at[rows], held.at[rows], sem.at[part])

    def store(part):
        rows = pl.ds(part * 8, 8)
        return pltpu.make_async_copy(held.at[rows], out.at[rows], sem.at[part])

    rest_fetch = pltpu.make_async_copy(last, rest, rest_sem)
    rest_fetch.start()
    for part in range(parts):
        fetch(part).start()
    label = label_of(labels, first, count)
    rest_fetch.wait()

    def add(part, carry):
        onehot = onehot_rows(label, part * 256, (256, count * CHIPS))
        fetch(part).wait()
        width = rest.shape[-1]
        for piece in range(rest.shape[0]):
            x, lanes = piece * width // B, piece * width % B
            lanes = slice(lanes, lanes + width)
            total = jnp.dot(
                onehot, rest[piece], preferred_element_type=jnp.float32
            ).reshape(8, SECTORS, width)
            total = total + held[pl.ds(part * 8, 8), x, :, lanes].astype(jnp.float32)
            held[pl.ds(part * 8, 8), x, :, lanes] = total.astype(jnp.bfloat16)
        store(part).start()
        return carry

    lax.fori_loop(0, parts, add, 0)
    for part in range(parts):
        store(part).wait()


def finished(slots, labels, partial, last):
    count = last_count(slots)
    anywhere = pl.BlockSpec(memory_space=pl.ANY)
    return pl.pallas_call(
        functools.partial(finish_kernel, slots - count, count),
        name=f"finish_{slots}",
        out_shape=jax.ShapeDtypeStruct(partial.shape, partial.dtype),
        in_specs=[pl.BlockSpec(memory_space=pltpu.VMEM), anywhere, anywhere],
        out_specs=anywhere,
        scratch_shapes=[
            pltpu.VMEM(partial.shape, partial.dtype),
            pltpu.VMEM(last.shape, last.dtype),
            pltpu.SemaphoreType.DMA((SECTORS // 8,)),
            pltpu.SemaphoreType.DMA,
        ],
        compiler_params=pltpu.CompilerParams(vmem_limit_bytes=VMEM_LIMIT),
        cost_estimate=pl.CostEstimate(
            flops=2 * SECTORS**2 * count * CHIPS * ROWS * B,
            bytes_accessed=9 * 2**20,
            transcendentals=0,
        ),
    )(labels, partial, last)


def local(psi, env_left, env_right, left_target, right_target, qn_left, qn_right):
    items, sources, labels, choice = tables(left_target, right_target, qn_left, qn_right)

    def branch(depth, slots, operands):
        labels = operands[2]
        return finished(slots, labels, *exchanged(depth, slots, *operands))

    return lax.switch(
        choice[0, 0],
        [functools.partial(branch, depth, slots) for depth, slots in SIZES],
        (items, sources, labels, psi, env_left, env_right),
    )


def solution(mesh):
    fine = Mesh(
        mesh.devices.reshape(CHIPS_Z, CORES, RIGHT), ("z", "core", "right")
    )
    left = ("z", "core")
    return jax.shard_map(
        local,
        mesh=fine,
        in_specs=(
            P(left, None, "right", None),
            P(None, left, None, None),
            P(None, "right", None, None),
            P(),
            P(),
            P(),
            P(),
        ),
        out_specs=P(None, ("z", "core", "right"), None, None),
        check_vma=False,
    )
```

```python
import functools

import jax
import jax.numpy as jnp
from jax import lax
from jax.experimental import pallas as pl
from jax.experimental.pallas import tpu as pltpu
from jax.sharding import Mesh, PartitionSpec as P

filling_charge = 3
B = 512
SECTORS = 32
TERMS = 2
CHIPS_Z = 4
CORES = 2
RIGHT = 16
CHIPS = CHIPS_Z * RIGHT
LEFT_DEV = SECTORS // (CHIPS_Z * CORES)
RIGHT_DEV = SECTORS // RIGHT
ITEMS = TERMS * LEFT_DEV * RIGHT_DEV
HALF = B // CORES
ROWS = B // (CHIPS * CORES)
MESH = pl.DeviceIdType.MESH
VMEM_LIMIT = 60 * 2**20
SIZES = ((10, 12), (10, 14), (12, 16), (12, 18), (16, 32))


def table_kernel(left_target, right_target, qn_left, qn_right, items, sources, labels, most):
    f32, bf16 = jnp.float32, jnp.bfloat16
    square = (SECTORS, SECTORS)
    row = lax.broadcasted_iota(jnp.int32, square, 0)
    column = lax.broadcasted_iota(jnp.int32, square, 1)
    wide = lambda value: value.astype(f32)
    dot = lambda a, b: jnp.dot(a.astype(bf16), b.astype(bf16), preferred_element_type=f32)
    upright = lambda line: jnp.sum(
        jnp.where(row == column, wide(line), 0.0), axis=1, keepdims=True
    )
    charge_left = qn_left[...]
    charge_right = upright(qn_right[...])

    pair = wide(row // RIGHT_DEV == column // RIGHT_DEV)
    second = wide((row + 1 == column) & (column % RIGHT_DEV == 1))
    same = row // LEFT_DEV == column // LEFT_DEV
    core = wide(row // LEFT_DEV % CORES)
    swap = wide(column == row + LEFT_DEV - 2 * LEFT_DEV * (row // LEFT_DEV % CORES))
    active, to_left, to_right, rank, total = [], [], [], [], []
    for t in range(TERMS):
        lefts = upright(left_target[t : t + 1, :])
        rights = wide(right_target[t : t + 1, :])
        hit_left = wide(column) == lefts
        hit_right = wide(row) == rights
        have_left = jnp.sum(jnp.where(hit_left, wide(charge_left), 0.0), axis=1, keepdims=True)
        have_right = jnp.sum(jnp.where(hit_right, charge_right, 0.0), axis=0, keepdims=True)
        allowed = have_left + have_right == float(filling_charge)
        ones = jnp.where(allowed, 1.0, 0.0)
        count = dot(ones, pair)
        active.append(allowed)
        to_left.append(lefts)
        to_right.append(rights)
        rank.append(dot(wide(same & (column < row)), count) + dot(ones, second))
        total.append(dot(wide(same), count))
    rank[1] = rank[1] + total[0]
    own = total[0] + total[1]
    other = dot(swap, own)
    slot = [r + jnp.minimum(other, r + core) for r in rank]

    lane = lax.broadcasted_iota(jnp.int32, (SECTORS, 128), 1)
    tall = lax.broadcasted_iota(jnp.int32, (SECTORS, 128), 0)
    device_lane = tall // RIGHT_DEV == lane % RIGHT
    device_row = tall // LEFT_DEV == lane // RIGHT
    chip_row = tall // (CORES * LEFT_DEV) == lane % CHIPS // RIGHT

    def spread(steps, place, values, rows):
        stack = []
        for k in steps:
            picked = jnp.zeros(square, f32)
            for t in range(TERMS):
                picked = picked + jnp.where(
                    active[t] & (place[t] == float(k)), values[t], 0.0
                )
            stack.append(picked.astype(bf16))
        lanes = dot(jnp.concatenate(stack, axis=0), wide(device_lane))
        lanes = lanes.reshape(len(stack), SECTORS, 128)
        return jnp.sum(jnp.where(rows[None], lanes, 0.0), axis=1)

    item = wide(row % LEFT_DEV * RIGHT_DEV + column % RIGHT_DEV)
    items[...] = spread(
        range(ITEMS), rank, [item, item + float(LEFT_DEV * RIGHT_DEV)], device_row
    ).astype(jnp.int32)

    half_lane = lax.broadcasted_iota(jnp.int32, (ITEMS, 128), 1)

    def by_slot(values):
        both = spread(
            [*range(0, 2 * ITEMS, 2), *range(1, 2 * ITEMS, 2)], slot, values, chip_row
        )
        return jnp.where(half_lane < CHIPS, both[:ITEMS], both[ITEMS:])

    sources[...] = by_slot([core * ITEMS + r for r in rank]).astype(jnp.int32)
    full = jnp.zeros(square, f32)
    high = by_slot([full + lefts + 1.0 for lefts in to_left])
    low = by_slot([full + rights for rights in to_right])
    labels[...] = ((high - 1.0) * SECTORS + low).astype(jnp.int32)
    most_device = jnp.max(own)
    most_chip = jnp.max(own + other)
    choice = jnp.int32(0)
    for depth, slots in SIZES[:-1]:
        choice = choice + jnp.where(
            (most_device > float(depth)) | (most_chip > float(slots)), 1, 0
        )
    most[0, 0] = choice


def tables(left_target, right_target, qn_left, qn_right):
    vmem = pl.BlockSpec(memory_space=pltpu.VMEM)
    table = jax.ShapeDtypeStruct((ITEMS, 128), jnp.int32)
    return pl.pallas_call(
        table_kernel,
        name="tables",
        out_shape=[table, table, table, jax.ShapeDtypeStruct((1, 1), jnp.int32)],
        in_specs=[vmem] * 4,
        out_specs=[vmem] * 3 + [pl.BlockSpec(memory_space=pltpu.SMEM)],
        cost_estimate=pl.CostEstimate(flops=2**24, bytes_accessed=2**15, transcendentals=0),
    )(
        left_target,
        right_target,
        qn_left.reshape(1, SECTORS),
        qn_right.reshape(1, SECTORS),
    )


def fours_of(slots):
    return (slots - 2) // 4


def last_count(slots):
    return 4 if slots % 4 == 2 else 2


def last_shape(count):
    return ROWS * 4 // count, count * CHIPS, B * count // 4


def onehot_rows(label, first, shape):
    row = first + lax.broadcasted_iota(jnp.int32, shape, 0)
    return jnp.where(row == label, 1.0, 0.0).astype(jnp.bfloat16)


def label_of(labels, first, count):
    return jnp.concatenate(
        [labels[pl.ds(first // 2 + p, 1), :] for p in range(count // 2)], axis=1
    )


def exchange(shape_from, shape_to):
    row = lax.broadcasted_iota(jnp.int32, (256, 256), 0)
    column = lax.broadcasted_iota(jnp.int32, (256, 256), 1)
    source = row % shape_from * shape_to + row // shape_from
    return jnp.where(column == source, 1.0, 0.0).astype(jnp.bfloat16)


def reorder(onehot, rows):
    return jnp.dot(onehot, rows, preferred_element_type=jnp.float32).astype(jnp.bfloat16)


def order(incoming, count, sorted_rows):
    unsort = exchange(16, 16)

    def sort(far_z, carry):
        rows = incoming[pl.ds(far_z * RIGHT, RIGHT)]
        rows = reorder(unsort, rows.reshape(256, rows.shape[-1]))
        for piece in range(16):
            start = pl.multiple_of(piece % count * CHIPS + far_z * RIGHT, RIGHT)
            sorted_rows[piece // count, pl.ds(start, RIGHT), :] = rows[
                piece * RIGHT : (piece + 1) * RIGHT
            ]
        return carry

    lax.fori_loop(0, CHIPS_Z, sort, 0, unroll=2)


def exchange_kernel(
    depth,
    slots,
    items,
    sources,
    labels,
    psi_hbm,
    left_hbm,
    right_hbm,
    out,
    last,
    landed,
    psi,
    left,
    right,
    product,
    both,
    send,
    arrived,
    send_pair,
    arrived_pair,
    partial,
    ordered,
    ordered_pair,
    in_sem,
    own_sem,
    pair_send_sem,
    pair_recv_sem,
    free_sem,
    self_sem,
    send_sem,
    recv_sem,
    out_sem,
):
    z = lax.axis_index("z")
    core = lax.axis_index("core")
    place = lax.axis_index("right")
    other = 1 - core
    partner = (z, other, place)
    here = z * RIGHT + place
    device = (z * CORES + core) * RIGHT + place
    fours = fours_of(slots)
    stages = -(-(depth + 2) // 4)
    ends_in_pair = last_count(slots) == 2

    psi_rows = psi_hbm.reshape(LEFT_DEV, B * RIGHT_DEV, B)
    psi_load = [
        pltpu.make_async_copy(psi_rows.at[a], landed.at[a], in_sem.at[a])
        for a in range(LEFT_DEV)
    ]
    left_load = pltpu.make_async_copy(left_hbm, left, in_sem.at[LEFT_DEV])
    right_load = pltpu.make_async_copy(right_hbm, right, in_sem.at[LEFT_DEV + 1])
    for load in (*psi_load, left_load, right_load):
        load.start()

    steps = (1, 3, 2, 0)
    way = 1 - 2 * core
    route = []
    for i in range(RIGHT):
        step_x = steps[i % 4]
        step_y = steps[(i + i // 4) % 4]
        far_x = (place // 4 + 4 + way * step_x) % 4
        far_y = (place % 4 + 4 + way * step_y) % 4
        route.append((step_x + step_y, steps[(i + i // 4 * 2) % 4], far_x * 4 + far_y))

    def for_others(visit):
        def turn(shift, carry):
            far_z = [
                (z + 2 * CHIPS_Z + way * (shift + step)) % CHIPS_Z for step in range(CHIPS_Z)
            ]
            for moved, step, far_place in route:
                if moved or step:
                    visit(far_z[step], far_place)
                else:
                    pl.when(shift > 0)(functools.partial(visit, far_z[step], far_place))
            return carry

        lax.fori_loop(0, CHIPS_Z, turn, 0)

    barrier = pltpu.get_barrier_semaphore()
    pl.semaphore_signal(barrier, inc=1, device_id=partner, device_id_type=MESH)

    def greet(far_z, far_place):
        pl.semaphore_signal(
            barrier, inc=1, device_id=(far_z, core, far_place), device_id_type=MESH
        )

    for_others(greet)

    unmix = exchange(128, RIGHT_DEV)

    def split(a, carry):
        for part in range(B // 128):
            apart = reorder(unmix, landed[a, part * 256 : part * 256 + 256, :])
            for b in range(RIGHT_DEV):
                psi[a * RIGHT_DEV + b, part * 128 : part * 128 + 128, :] = apart[
                    b * 128 : (b + 1) * 128
                ]
        return carry

    psi_load[0].wait()
    split(0, 0)

    def next_split(a, carry):
        pltpu.make_async_copy(psi_rows.at[a], landed.at[a], in_sem.at[a]).wait()
        return split(a, carry)

    lax.fori_loop(1, LEFT_DEV, next_split, 0)
    left_load.wait()
    right_load.wait()

    def own_copy(rank):
        return pltpu.make_async_copy(
            product.at[rank, :, core], both.at[core * depth + rank], own_sem.at[rank]
        )

    def pair_copy(rank):
        return pltpu.make_async_remote_copy(
            src_ref=product.at[rank, :, other],
            dst_ref=both.at[core * depth + rank],
            send_sem=pair_send_sem.at[rank],
            recv_sem=pair_recv_sem.at[rank],
            device_id=partner,
            device_id_type=MESH,
        )

    def multiply_two(step):
        ranks = (2 * step, 2 * step + 1)
        halves, rights = [], []
        for rank in ranks:
            item = items[rank, device]
            term = item // (LEFT_DEV * RIGHT_DEV)
            pair = item % (LEFT_DEV * RIGHT_DEV)
            half = jnp.dot(
                left[term * LEFT_DEV + pair // RIGHT_DEV],
                psi[pair],
                preferred_element_type=jnp.float32,
            )
            halves.append(half.astype(jnp.bfloat16))
            rights.append(right[term * RIGHT_DEV + pair % RIGHT_DEV])
        for rank, half, by in zip(ranks, halves, rights):
            moved = lax.dot_general(
                half, by, (((1,), (1,)), ((), ())), preferred_element_type=jnp.float32
            ).astype(jnp.bfloat16)
            product[rank] = moved.reshape(CHIPS_Z, CORES, B // (CHIPS_Z * CORES), B)

    def swap_two(step):
        @pl.when(step == 0)
        def _():
            pl.semaphore_wait(barrier, CHIPS)

        @pl.when((step > 0) & (step % 2 == 1))
        def _():
            pl.semaphore_wait(free_sem, 1)

        for rank in (2 * step, 2 * step + 1):
            pair_copy(rank).start()
            own_copy(rank).start()

    def advance(step, carry):
        pl.when(step >= 0)(lambda: swap_two(step))
        pl.when(step + 1 < depth // 2)(lambda: multiply_two(step + 1))
        return carry

    def arrive(rank, carry):
        own_copy(rank).wait()
        pair_copy(rank).wait_recv()
        return carry

    def departing(outgoing, incoming, chunk, far_z, far_place):
        pltpu.make_async_remote_copy(
            src_ref=outgoing.at[far_z * RIGHT + far_place],
            dst_ref=incoming.at[here],
            send_sem=send_sem.at[chunk],
            recv_sem=recv_sem.at[chunk],
            device_id=(far_z, core, far_place),
            device_id_type=MESH,
        ).start()

    def self_copy(outgoing, incoming, chunk):
        return pltpu.make_async_copy(
            outgoing.at[here], incoming.at[here], self_sem.at[chunk]
        )

    mix = exchange(4, 64)

    def pack(outgoing, first, count):
        def quarter(far_z, carry):
            def block(k):
                source = sources[first // 2 + k // 2, k % 2 * CHIPS + here]
                return both[source // ITEMS * depth + source % ITEMS, far_z]

            blocks = [block(k) for k in range(count)]
            if count == 2:
                blocks = [rows[:, : B // 2] for rows in blocks] + [rows[:, B // 2 :] for rows in blocks]
            rows = reorder(mix, jnp.concatenate(blocks, axis=0))
            outgoing[pl.ds(far_z * RIGHT, RIGHT)] = rows.reshape(
                RIGHT, 4 * ROWS, rows.shape[-1]
            )
            return carry

        lax.fori_loop(0, CHIPS_Z, quarter, 0, unroll=2)

    def depart(outgoing, incoming, chunk):
        self_copy(outgoing, incoming, chunk).start()
        for_others(functools.partial(departing, outgoing, incoming, chunk))

    def stage(turn, carry):
        start = jnp.maximum(4 * turn - 2, 0)
        stop = jnp.maximum(jnp.minimum(4 * turn + 2, depth), start)
        lax.fori_loop(jnp.where(turn == 0, -1, start // 2), stop // 2, advance, 0)
        lax.fori_loop(start, stop, arrive, 0)

        four = jnp.maximum(turn - 1, 0)
        pl.when(turn == 0)(lambda: pack(send_pair.at[0], 0, 2))
        pl.when(turn > 0)(lambda: pack(send.at[four], 2 + 4 * four, 4))

        @pl.when(turn < stages - 1)
        def _():
            pl.semaphore_signal(free_sem, inc=1, device_id=partner, device_id_type=MESH)

        pl.when(turn == 0)(lambda: depart(send_pair.at[0], arrived_pair.at[0], fours))
        pl.when(turn > 0)(lambda: depart(send.at[four], arrived.at[four], four))
        return carry

    lax.fori_loop(0, fours + 1, stage, 0)
    if ends_in_pair:
        pack(send_pair.at[1], slots - 2, 2)
        depart(send_pair.at[1], arrived_pair.at[1], fours + 1)

    def receive(outgoing, incoming, chunk):
        self_copy(outgoing, incoming, chunk).wait()
        arrivals = incoming.at[pl.ds(0, CHIPS - 1)]
        pltpu.make_async_copy(arrivals, arrivals, recv_sem.at[chunk]).wait()

    partial[...] = jnp.zeros(partial.shape, partial.dtype)

    def place_chunk(first, count, sorted_rows):
        label = label_of(labels, first, count)
        pieces, _, width = sorted_rows.shape

        def put(part, carry):
            onehot = onehot_rows(label, part * 256, (256, count * CHIPS))

            def row(x, carry):
                for half in range(pieces // ROWS):
                    lanes = slice(half * width, half * width + width)
                    total = jnp.dot(
                        onehot,
                        sorted_rows[x * (pieces // ROWS) + half],
                        preferred_element_type=jnp.float32,
                    ).reshape(8, SECTORS, width)
                    total = total + partial[pl.ds(part * 8, 8), x, :, lanes].astype(jnp.float32)
                    partial[pl.ds(part * 8, 8), x, :, lanes] = total.astype(jnp.bfloat16)
                return carry

            return lax.fori_loop(0, ROWS, row, carry, unroll=2)

        lax.fori_loop(0, SECTORS // 8, put, 0)

    receive(send_pair.at[0], arrived_pair.at[0], fours)
    order(arrived_pair.at[0], 2, ordered_pair)
    place_chunk(0, 2, ordered_pair)
    placed = fours if ends_in_pair else fours - 1

    def collect(four, carry):
        receive(send.at[four], arrived.at[four], four)
        order(arrived.at[four], 4, ordered)

        @pl.when(four < placed)
        def _():
            place_chunk(2 + 4 * four, 4, ordered)

        @pl.when(four == placed - 1)
        def _():
            pltpu.make_async_copy(partial, out, out_sem.at[0]).start()

        return carry

    lax.fori_loop(0, fours, collect, 0)
    rest = ordered
    if ends_in_pair:
        receive(send_pair.at[1], arrived_pair.at[1], fours + 1)
        order(arrived_pair.at[1], 2, ordered_pair)
        rest = ordered_pair
    rest_out = pltpu.make_async_copy(rest, last, out_sem.at[1])
    rest_out.start()

    def sent(rank, carry):
        pair_copy(rank).wait_send()
        return carry

    lax.fori_loop(0, depth, sent, 0)

    def gone(chunk, carry):
        departures = send.at[chunk, pl.ds(0, CHIPS - 1)]
        pltpu.make_async_copy(departures, departures, send_sem.at[chunk]).wait()
        return carry

    lax.fori_loop(0, fours, gone, 0)
    for pair in range(1 + ends_in_pair):
        departures = send_pair.at[pair, pl.ds(0, CHIPS - 1)]
        pltpu.make_async_copy(departures, departures, send_sem.at[fours + pair]).wait()
    pltpu.make_async_copy(partial, out, out_sem.at[0]).wait()
    rest_out.wait()


def exchanged(depth, slots, items, sources, labels, psi, env_left, env_right):
    smem = pl.BlockSpec(memory_space=pltpu.SMEM)
    anywhere = pl.BlockSpec(memory_space=pl.ANY)
    vmem = pl.BlockSpec(memory_space=pltpu.VMEM)
    bf16 = jnp.bfloat16
    fours = fours_of(slots)
    messages = (CHIPS, 4 * ROWS, B)
    pair_messages = (2, CHIPS, 4 * ROWS, B // 2)
    dma = pltpu.SemaphoreType.DMA
    return pl.pallas_call(
        functools.partial(exchange_kernel, depth, slots),
        name=f"exchange_{slots}",
        out_shape=[
            jax.ShapeDtypeStruct((SECTORS, ROWS, SECTORS, B), bf16),
            jax.ShapeDtypeStruct(last_shape(last_count(slots)), bf16),
        ],
        in_specs=[smem] * 2 + [vmem] + [anywhere] * 3,
        out_specs=[anywhere] * 2,
        scratch_shapes=[
            pltpu.VMEM((LEFT_DEV, B * RIGHT_DEV, B), bf16),
            pltpu.VMEM((LEFT_DEV * RIGHT_DEV, B, B), bf16),
            pltpu.VMEM((TERMS * LEFT_DEV, B, B), bf16),
            pltpu.VMEM((TERMS * RIGHT_DEV, B, B), bf16),
            pltpu.VMEM((depth, CHIPS_Z, CORES, B // (CHIPS_Z * CORES), B), bf16),
            pltpu.VMEM((CORES * depth, CHIPS_Z, B // (CHIPS_Z * CORES), B), bf16),
            pltpu.VMEM((fours, *messages), bf16),
            pltpu.VMEM((fours, *messages), bf16),
            pltpu.VMEM(pair_messages, bf16),
            pltpu.VMEM(pair_messages, bf16),
            pltpu.VMEM((SECTORS, ROWS, SECTORS, B), bf16),
            pltpu.VMEM(last_shape(4), bf16),
            pltpu.VMEM(last_shape(2), bf16),
            dma((LEFT_DEV + 2,)),
            dma((depth,)),
            dma((depth,)),
            dma((depth,)),
            pltpu.SemaphoreType.REGULAR,
            dma((fours + 2,)),
            dma((fours + 2,)),
            dma((fours + 2,)),
            dma((2,)),
        ],
        compiler_params=pltpu.CompilerParams(
            collective_id=slots // 2,
            has_side_effects=True,
            vmem_limit_bytes=VMEM_LIMIT,
        ),
        cost_estimate=pl.CostEstimate(
            flops=4 * depth * B**3, bytes_accessed=14 * 2**20, transcendentals=0
        ),
    )(
        items,
        sources,
        labels,
        psi,
        env_left.reshape(TERMS * LEFT_DEV, B, B),
        env_right.reshape(TERMS * RIGHT_DEV, B, B),
    )


def finish_kernel(first, count, labels, partial, last, out, held, rest, sem, rest_sem):
    parts = held.shape[0] // 8

    def fetch(part):
        rows = pl.ds(part * 8, 8)
        return pltpu.make_async_copy(partial.at[rows], held.at[rows], sem.at[part])

    def store(part):
        rows = pl.ds(part * 8, 8)
        return pltpu.make_async_copy(held.at[rows], out.at[rows], sem.at[part])

    rest_fetch = pltpu.make_async_copy(last, rest, rest_sem)
    rest_fetch.start(priority=1)
    for part in range(parts):
        fetch(part).start()
    label = label_of(labels, first, count)
    rest_fetch.wait()

    def add(part, carry):
        onehot = onehot_rows(label, part * 256, (256, count * CHIPS))
        fetch(part).wait()
        width = rest.shape[-1]
        for piece in range(rest.shape[0]):
            x, lanes = piece * width // B, piece * width % B
            lanes = slice(lanes, lanes + width)
            total = jnp.dot(
                onehot, rest[piece], preferred_element_type=jnp.float32
            ).reshape(8, SECTORS, width)
            total = total + held[pl.ds(part * 8, 8), x, :, lanes].astype(jnp.float32)
            held[pl.ds(part * 8, 8), x, :, lanes] = total.astype(jnp.bfloat16)
        store(part).start()
        return carry

    lax.fori_loop(0, parts, add, 0)
    for part in range(parts):
        store(part).wait()


def finished(slots, labels, partial, last):
    count = last_count(slots)
    anywhere = pl.BlockSpec(memory_space=pl.ANY)
    return pl.pallas_call(
        functools.partial(finish_kernel, slots - count, count),
        name=f"finish_{slots}",
        out_shape=jax.ShapeDtypeStruct(partial.shape, partial.dtype),
        in_specs=[pl.BlockSpec(memory_space=pltpu.VMEM), anywhere, anywhere],
        out_specs=anywhere,
        scratch_shapes=[
            pltpu.VMEM(partial.shape, partial.dtype),
            pltpu.VMEM(last.shape, last.dtype),
            pltpu.SemaphoreType.DMA((SECTORS // 8,)),
            pltpu.SemaphoreType.DMA,
        ],
        compiler_params=pltpu.CompilerParams(vmem_limit_bytes=VMEM_LIMIT),
        cost_estimate=pl.CostEstimate(
            flops=2 * SECTORS**2 * count * CHIPS * ROWS * B,
            bytes_accessed=9 * 2**20,
            transcendentals=0,
        ),
    )(labels, partial, last)


def local(psi, env_left, env_right, left_target, right_target, qn_left, qn_right):
    items, sources, labels, choice = tables(left_target, right_target, qn_left, qn_right)

    def branch(depth, slots, operands):
        labels = operands[2]
        return finished(slots, labels, *exchanged(depth, slots, *operands))

    return lax.switch(
        choice[0, 0],
        [functools.partial(branch, depth, slots) for depth, slots in SIZES],
        (items, sources, labels, psi, env_left, env_right),
    )


def solution(mesh):
    fine = Mesh(
        mesh.devices.reshape(CHIPS_Z, CORES, RIGHT), ("z", "core", "right")
    )
    left = ("z", "core")
    return jax.shard_map(
        local,
        mesh=fine,
        in_specs=(
            P(left, None, "right", None),
            P(None, left, None, None),
            P(None, "right", None, None),
            P(),
            P(),
            P(),
            P(),
        ),
        out_specs=P(None, ("z", "core", "right"), None, None),
        check_vma=False,
    )
```

```python
import functools

import jax
import jax.numpy as jnp
from jax import lax
from jax.experimental import pallas as pl
from jax.experimental.pallas import tpu as pltpu
from jax.sharding import Mesh, PartitionSpec as P

filling_charge = 3
B = 512
SECTORS = 32
TERMS = 2
CHIPS_Z = 4
CORES = 2
RIGHT = 16
CHIPS = CHIPS_Z * RIGHT
LEFT_DEV = SECTORS // (CHIPS_Z * CORES)
RIGHT_DEV = SECTORS // RIGHT
ITEMS = TERMS * LEFT_DEV * RIGHT_DEV
HALF = B // CORES
ROWS = B // (CHIPS * CORES)
MESH = pl.DeviceIdType.MESH
VMEM_LIMIT = 60 * 2**20
SIZES = ((10, 12), (10, 14), (12, 16), (12, 18), (16, 32))


def table_kernel(left_target, right_target, qn_left, qn_right, items, sources, labels, most):
    f32, bf16 = jnp.float32, jnp.bfloat16
    square = (SECTORS, SECTORS)
    row = lax.broadcasted_iota(jnp.int32, square, 0)
    column = lax.broadcasted_iota(jnp.int32, square, 1)
    wide = lambda value: value.astype(f32)
    dot = lambda a, b: jnp.dot(a.astype(bf16), b.astype(bf16), preferred_element_type=f32)
    upright = lambda line: jnp.sum(
        jnp.where(row == column, wide(line), 0.0), axis=1, keepdims=True
    )
    charge_left = qn_left[...]
    charge_right = upright(qn_right[...])

    pair = wide(row // RIGHT_DEV == column // RIGHT_DEV)
    second = wide((row + 1 == column) & (column % RIGHT_DEV == 1))
    same = row // LEFT_DEV == column // LEFT_DEV
    core = wide(row // LEFT_DEV % CORES)
    swap = wide(column == row + LEFT_DEV - 2 * LEFT_DEV * (row // LEFT_DEV % CORES))
    active, to_left, to_right, rank, total = [], [], [], [], []
    for t in range(TERMS):
        lefts = upright(left_target[t : t + 1, :])
        rights = wide(right_target[t : t + 1, :])
        hit_left = wide(column) == lefts
        hit_right = wide(row) == rights
        have_left = jnp.sum(jnp.where(hit_left, wide(charge_left), 0.0), axis=1, keepdims=True)
        have_right = jnp.sum(jnp.where(hit_right, charge_right, 0.0), axis=0, keepdims=True)
        allowed = have_left + have_right == float(filling_charge)
        ones = jnp.where(allowed, 1.0, 0.0)
        count = dot(ones, pair)
        active.append(allowed)
        to_left.append(lefts)
        to_right.append(rights)
        rank.append(dot(wide(same & (column < row)), count) + dot(ones, second))
        total.append(dot(wide(same), count))
    rank[1] = rank[1] + total[0]
    own = total[0] + total[1]
    other = dot(swap, own)
    slot = [r + jnp.minimum(other, r + core) for r in rank]

    lane = lax.broadcasted_iota(jnp.int32, (SECTORS, 128), 1)
    tall = lax.broadcasted_iota(jnp.int32, (SECTORS, 128), 0)
    device_lane = tall // RIGHT_DEV == lane % RIGHT
    device_row = tall // LEFT_DEV == lane // RIGHT
    chip_row = tall // (CORES * LEFT_DEV) == lane % CHIPS // RIGHT

    def spread(steps, place, values, rows):
        stack = []
        for k in steps:
            picked = jnp.zeros(square, f32)
            for t in range(TERMS):
                picked = picked + jnp.where(
                    active[t] & (place[t] == float(k)), values[t], 0.0
                )
            stack.append(picked.astype(bf16))
        lanes = dot(jnp.concatenate(stack, axis=0), wide(device_lane))
        lanes = lanes.reshape(len(stack), SECTORS, 128)
        return jnp.sum(jnp.where(rows[None], lanes, 0.0), axis=1)

    item = wide(row % LEFT_DEV * RIGHT_DEV + column % RIGHT_DEV)
    items[...] = spread(
        range(ITEMS), rank, [item, item + float(LEFT_DEV * RIGHT_DEV)], device_row
    ).astype(jnp.int32)

    half_lane = lax.broadcasted_iota(jnp.int32, (ITEMS, 128), 1)

    def by_slot(values):
        both = spread(
            [*range(0, 2 * ITEMS, 2), *range(1, 2 * ITEMS, 2)], slot, values, chip_row
        )
        return jnp.where(half_lane < CHIPS, both[:ITEMS], both[ITEMS:])

    sources[...] = by_slot([core * ITEMS + r for r in rank]).astype(jnp.int32)
    full = jnp.zeros(square, f32)
    high = by_slot([full + lefts + 1.0 for lefts in to_left])
    low = by_slot([full + rights for rights in to_right])
    labels[...] = ((high - 1.0) * SECTORS + low).astype(jnp.int32)
    most_device = jnp.max(own)
    most_chip = jnp.max(own + other)
    choice = jnp.int32(0)
    for depth, slots in SIZES[:-1]:
        choice = choice + jnp.where(
            (most_device > float(depth)) | (most_chip > float(slots)), 1, 0
        )
    most[0, 0] = choice


def tables(left_target, right_target, qn_left, qn_right):
    vmem = pl.BlockSpec(memory_space=pltpu.VMEM)
    table = jax.ShapeDtypeStruct((ITEMS, 128), jnp.int32)
    return pl.pallas_call(
        table_kernel,
        name="tables",
        out_shape=[table, table, table, jax.ShapeDtypeStruct((1, 1), jnp.int32)],
        in_specs=[vmem] * 4,
        out_specs=[vmem] * 3 + [pl.BlockSpec(memory_space=pltpu.SMEM)],
        cost_estimate=pl.CostEstimate(flops=2**24, bytes_accessed=2**15, transcendentals=0),
    )(
        left_target,
        right_target,
        qn_left.reshape(1, SECTORS),
        qn_right.reshape(1, SECTORS),
    )


def fours_of(slots):
    return (slots - 2) // 4


def last_count(slots):
    return 4 if slots % 4 == 2 else 2


def last_shape(count):
    return ROWS * 4 // count, count * CHIPS, B * count // 4


def onehot_rows(label, first, shape):
    row = first + lax.broadcasted_iota(jnp.int32, shape, 0)
    return jnp.where(row == label, 1.0, 0.0).astype(jnp.bfloat16)


def label_of(labels, first, count):
    return jnp.concatenate(
        [labels[pl.ds(first // 2 + p, 1), :] for p in range(count // 2)], axis=1
    )


def exchange(shape_from, shape_to):
    row = lax.broadcasted_iota(jnp.int32, (256, 256), 0)
    column = lax.broadcasted_iota(jnp.int32, (256, 256), 1)
    source = row % shape_from * shape_to + row // shape_from
    return jnp.where(column == source, 1.0, 0.0).astype(jnp.bfloat16)


def reorder(onehot, rows):
    return jnp.dot(onehot, rows, preferred_element_type=jnp.float32).astype(jnp.bfloat16)


def order(incoming, count, sorted_rows):
    unsort = exchange(16, 16)

    def sort(far_z, carry):
        rows = incoming[pl.ds(far_z * RIGHT, RIGHT)]
        rows = reorder(unsort, rows.reshape(256, rows.shape[-1]))
        for piece in range(16):
            start = pl.multiple_of(piece % count * CHIPS + far_z * RIGHT, RIGHT)
            sorted_rows[piece // count, pl.ds(start, RIGHT), :] = rows[
                piece * RIGHT : (piece + 1) * RIGHT
            ]
        return carry

    lax.fori_loop(0, CHIPS_Z, sort, 0, unroll=2)


def exchange_kernel(
    depth,
    slots,
    items,
    sources,
    labels,
    psi_hbm,
    left_hbm,
    right_hbm,
    out,
    last,
    landed,
    psi,
    left,
    right,
    product,
    both_first,
    both,
    send,
    arrived,
    send_pair,
    arrived_pair,
    partial,
    ordered,
    ordered_pair,
    in_sem,
    own_sem,
    pair_send_sem,
    pair_recv_sem,
    free_sem,
    self_sem,
    send_sem,
    recv_sem,
    out_sem,
):
    z = lax.axis_index("z")
    core = lax.axis_index("core")
    place = lax.axis_index("right")
    other = 1 - core
    partner = (z, other, place)
    here = z * RIGHT + place
    device = (z * CORES + core) * RIGHT + place
    fours = fours_of(slots)
    ends_in_pair = last_count(slots) == 2

    psi_rows = psi_hbm.reshape(LEFT_DEV, B * RIGHT_DEV, B)
    psi_load = [
        pltpu.make_async_copy(psi_rows.at[a], landed.at[a], in_sem.at[a])
        for a in range(LEFT_DEV)
    ]
    left_load = pltpu.make_async_copy(left_hbm, left, in_sem.at[LEFT_DEV])
    right_load = pltpu.make_async_copy(right_hbm, right, in_sem.at[LEFT_DEV + 1])
    for load in (*psi_load, left_load, right_load):
        load.start()

    steps = (1, 3, 2, 0)
    way = 1 - 2 * core
    route = []
    for i in range(RIGHT):
        step_x = steps[i % 4]
        step_y = steps[(i + i // 4) % 4]
        far_x = (place // 4 + 4 + way * step_x) % 4
        far_y = (place % 4 + 4 + way * step_y) % 4
        route.append((step_x + step_y, steps[(i + i // 4 * 2) % 4], far_x * 4 + far_y))

    def for_others(visit):
        def turn(shift, carry):
            far_z = [
                (z + 2 * CHIPS_Z + way * (shift + step)) % CHIPS_Z for step in range(CHIPS_Z)
            ]
            for moved, step, far_place in route:
                if moved or step:
                    visit(far_z[step], far_place)
                else:
                    pl.when(shift > 0)(functools.partial(visit, far_z[step], far_place))
            return carry

        lax.fori_loop(0, CHIPS_Z, turn, 0)

    barrier = pltpu.get_barrier_semaphore()
    pl.semaphore_signal(barrier, inc=1, device_id=partner, device_id_type=MESH)

    def greet(far_z, far_place):
        pl.semaphore_signal(
            barrier, inc=1, device_id=(far_z, core, far_place), device_id_type=MESH
        )

    for_others(greet)

    unmix = exchange(128, RIGHT_DEV)

    def split(a, carry):
        for part in range(B // 128):
            apart = reorder(unmix, landed[a, part * 256 : part * 256 + 256, :])
            for b in range(RIGHT_DEV):
                psi[a * RIGHT_DEV + b, part * 128 : part * 128 + 128, :] = apart[
                    b * 128 : (b + 1) * 128
                ]
        return carry

    psi_load[0].wait()
    split(0, 0)

    def next_split(a, carry):
        pltpu.make_async_copy(psi_rows.at[a], landed.at[a], in_sem.at[a]).wait()
        return split(a, carry)

    lax.fori_loop(1, LEFT_DEV, next_split, 0)
    left_load.wait()
    right_load.wait()

    def half_of(rank, first):
        if first:
            return both_first.at[core * 2 + rank]
        return both.at[core * (depth - 2) + rank - 2]

    def own_copy(rank, first):
        return pltpu.make_async_copy(
            product.at[rank, :, core], half_of(rank, first), own_sem.at[rank]
        )

    def pair_copy(rank, first):
        return pltpu.make_async_remote_copy(
            src_ref=product.at[rank, :, other],
            dst_ref=half_of(rank, first),
            send_sem=pair_send_sem.at[rank],
            recv_sem=pair_recv_sem.at[rank],
            device_id=partner,
            device_id_type=MESH,
        )

    def multiply_two(step, carry):
        ranks = (2 * step, 2 * step + 1)
        halves, rights = [], []
        for rank in ranks:
            item = items[rank, device]
            term = item // (LEFT_DEV * RIGHT_DEV)
            pair = item % (LEFT_DEV * RIGHT_DEV)
            half = jnp.dot(
                left[term * LEFT_DEV + pair // RIGHT_DEV],
                psi[pair],
                preferred_element_type=jnp.float32,
            )
            halves.append(half.astype(jnp.bfloat16))
            rights.append(right[term * RIGHT_DEV + pair % RIGHT_DEV])
        for rank, half, by in zip(ranks, halves, rights):
            moved = lax.dot_general(
                half, by, (((1,), (1,)), ((), ())), preferred_element_type=jnp.float32
            ).astype(jnp.bfloat16)
            product[rank] = moved.reshape(CHIPS_Z, CORES, B // (CHIPS_Z * CORES), B)

        return carry

    def swap(rank, first):
        pair_copy(rank, first).start()
        own_copy(rank, first).start()

    def arrive(rank, first):
        own_copy(rank, first).wait()
        pair_copy(rank, first).wait_recv()

    def for_ranks(start, stop, visit):
        def one(rank, carry):
            visit(rank, False)
            return carry

        lax.fori_loop(start, stop, one, 0)

    def departing(outgoing, incoming, chunk, far_z, far_place):
        pltpu.make_async_remote_copy(
            src_ref=outgoing.at[far_z * RIGHT + far_place],
            dst_ref=incoming.at[here],
            send_sem=send_sem.at[chunk],
            recv_sem=recv_sem.at[chunk],
            device_id=(far_z, core, far_place),
            device_id_type=MESH,
        ).start()

    def self_copy(outgoing, incoming, chunk):
        return pltpu.make_async_copy(
            outgoing.at[here], incoming.at[here], self_sem.at[chunk]
        )

    mix = exchange(4, 64)

    def pack(outgoing, first, count, early=False):
        def quarter(far_z, carry):
            def block(k):
                source = sources[first // 2 + k // 2, k % 2 * CHIPS + here]
                of_core, rank = source // ITEMS, source % ITEMS
                rows = both_first[of_core * 2 + jnp.minimum(rank, 1), far_z]
                if early:
                    return rows
                later = both[of_core * (depth - 2) + jnp.maximum(rank - 2, 0), far_z]
                return jnp.where(rank < 2, rows, later)

            blocks = [block(k) for k in range(count)]
            if count == 2:
                blocks = [rows[:, : B // 2] for rows in blocks] + [rows[:, B // 2 :] for rows in blocks]
            rows = reorder(mix, jnp.concatenate(blocks, axis=0))
            outgoing[pl.ds(far_z * RIGHT, RIGHT)] = rows.reshape(
                RIGHT, 4 * ROWS, rows.shape[-1]
            )
            return carry

        lax.fori_loop(0, CHIPS_Z, quarter, 0, unroll=2)

    def depart(outgoing, incoming, chunk):
        self_copy(outgoing, incoming, chunk).start()
        for_others(functools.partial(departing, outgoing, incoming, chunk))

    steps_all = depth // 2

    def stage(turn, carry):
        start = jnp.where(turn == 0, 0, jnp.minimum(2 * turn + 1, steps_all))
        stop = jnp.minimum(2 * turn + 3, steps_all)
        lax.fori_loop(start, stop, multiply_two, 0)
        four = jnp.maximum(turn - 1, 0)

        @pl.when(turn == 0)
        def _():
            pl.semaphore_wait(barrier, CHIPS)
            for rank in range(2):
                swap(rank, True)
            for_ranks(2, 6, swap)
            for rank in range(2):
                arrive(rank, True)
            pack(send_pair.at[0], 0, 2, early=True)
            depart(send_pair.at[0], arrived_pair.at[0], fours)

        @pl.when(turn > 0)
        def _():
            here_from = jnp.minimum(4 * turn - 2, depth)
            for_ranks(here_from, jnp.minimum(4 * turn + 2, depth), arrive)
            pack(send.at[four], 2 + 4 * four, 4)

            @pl.when(start < stop)
            def _():
                pl.semaphore_signal(free_sem, inc=1, device_id=partner, device_id_type=MESH)
                pl.semaphore_wait(free_sem, 1)
                for_ranks(2 * start, 2 * stop, swap)

            depart(send.at[four], arrived.at[four], four)

        return carry

    lax.fori_loop(0, fours + 1, stage, 0)
    if ends_in_pair:
        pack(send_pair.at[1], slots - 2, 2)
        depart(send_pair.at[1], arrived_pair.at[1], fours + 1)

    def receive(outgoing, incoming, chunk):
        self_copy(outgoing, incoming, chunk).wait()
        arrivals = incoming.at[pl.ds(0, CHIPS - 1)]
        pltpu.make_async_copy(arrivals, arrivals, recv_sem.at[chunk]).wait()

    partial[...] = jnp.zeros(partial.shape, partial.dtype)

    def place_chunk(first, count, sorted_rows):
        label = label_of(labels, first, count)
        pieces, _, width = sorted_rows.shape

        def put(part, carry):
            onehot = onehot_rows(label, part * 256, (256, count * CHIPS))

            def row(x, carry):
                for half in range(pieces // ROWS):
                    lanes = slice(half * width, half * width + width)
                    total = jnp.dot(
                        onehot,
                        sorted_rows[x * (pieces // ROWS) + half],
                        preferred_element_type=jnp.float32,
                    ).reshape(8, SECTORS, width)
                    total = total + partial[pl.ds(part * 8, 8), x, :, lanes].astype(jnp.float32)
                    partial[pl.ds(part * 8, 8), x, :, lanes] = total.astype(jnp.bfloat16)
                return carry

            return lax.fori_loop(0, ROWS, row, carry, unroll=2)

        lax.fori_loop(0, SECTORS // 8, put, 0)

    receive(send_pair.at[0], arrived_pair.at[0], fours)
    order(arrived_pair.at[0], 2, ordered_pair)
    place_chunk(0, 2, ordered_pair)
    placed = fours if ends_in_pair else fours - 1

    def collect(four, carry):
        receive(send.at[four], arrived.at[four], four)
        order(arrived.at[four], 4, ordered)

        @pl.when(four < placed)
        def _():
            place_chunk(2 + 4 * four, 4, ordered)

        @pl.when(four == placed - 1)
        def _():
            pltpu.make_async_copy(partial, out, out_sem.at[0]).start()

        return carry

    lax.fori_loop(0, fours, collect, 0)
    rest = ordered
    if ends_in_pair:
        receive(send_pair.at[1], arrived_pair.at[1], fours + 1)
        order(arrived_pair.at[1], 2, ordered_pair)
        rest = ordered_pair
    rest_out = pltpu.make_async_copy(rest, last, out_sem.at[1])
    rest_out.start()

    for rank in range(2):
        pair_copy(rank, True).wait_send()
    for_ranks(2, depth, lambda rank, first: pair_copy(rank, first).wait_send())

    def gone(chunk, carry):
        departures = send.at[chunk, pl.ds(0, CHIPS - 1)]
        pltpu.make_async_copy(departures, departures, send_sem.at[chunk]).wait()
        return carry

    lax.fori_loop(0, fours, gone, 0)
    for pair in range(1 + ends_in_pair):
        departures = send_pair.at[pair, pl.ds(0, CHIPS - 1)]
        pltpu.make_async_copy(departures, departures, send_sem.at[fours + pair]).wait()
    pltpu.make_async_copy(partial, out, out_sem.at[0]).wait()
    rest_out.wait()


def exchanged(depth, slots, items, sources, labels, psi, env_left, env_right):
    smem = pl.BlockSpec(memory_space=pltpu.SMEM)
    anywhere = pl.BlockSpec(memory_space=pl.ANY)
    vmem = pl.BlockSpec(memory_space=pltpu.VMEM)
    bf16 = jnp.bfloat16
    fours = fours_of(slots)
    messages = (CHIPS, 4 * ROWS, B)
    pair_messages = (2, CHIPS, 4 * ROWS, B // 2)
    dma = pltpu.SemaphoreType.DMA
    return pl.pallas_call(
        functools.partial(exchange_kernel, depth, slots),
        name=f"exchange_{slots}",
        out_shape=[
            jax.ShapeDtypeStruct((SECTORS, ROWS, SECTORS, B), bf16),
            jax.ShapeDtypeStruct(last_shape(last_count(slots)), bf16),
        ],
        in_specs=[smem] * 2 + [vmem] + [anywhere] * 3,
        out_specs=[anywhere] * 2,
        scratch_shapes=[
            pltpu.VMEM((LEFT_DEV, B * RIGHT_DEV, B), bf16),
            pltpu.VMEM((LEFT_DEV * RIGHT_DEV, B, B), bf16),
            pltpu.VMEM((TERMS * LEFT_DEV, B, B), bf16),
            pltpu.VMEM((TERMS * RIGHT_DEV, B, B), bf16),
            pltpu.VMEM((depth, CHIPS_Z, CORES, B // (CHIPS_Z * CORES), B), bf16),
            pltpu.VMEM((CORES * 2, CHIPS_Z, B // (CHIPS_Z * CORES), B), bf16),
            pltpu.VMEM((CORES * (depth - 2), CHIPS_Z, B // (CHIPS_Z * CORES), B), bf16),
            pltpu.VMEM((fours, *messages), bf16),
            pltpu.VMEM((fours, *messages), bf16),
            pltpu.VMEM(pair_messages, bf16),
            pltpu.VMEM(pair_messages, bf16),
            pltpu.VMEM((SECTORS, ROWS, SECTORS, B), bf16),
            pltpu.VMEM(last_shape(4), bf16),
            pltpu.VMEM(last_shape(2), bf16),
            dma((LEFT_DEV + 2,)),
            dma((depth,)),
            dma((depth,)),
            dma((depth,)),
            pltpu.SemaphoreType.REGULAR,
            dma((fours + 2,)),
            dma((fours + 2,)),
            dma((fours + 2,)),
            dma((2,)),
        ],
        compiler_params=pltpu.CompilerParams(
            collective_id=slots // 2,
            has_side_effects=True,
            vmem_limit_bytes=VMEM_LIMIT,
        ),
        cost_estimate=pl.CostEstimate(
            flops=4 * depth * B**3, bytes_accessed=14 * 2**20, transcendentals=0
        ),
    )(
        items,
        sources,
        labels,
        psi,
        env_left.reshape(TERMS * LEFT_DEV, B, B),
        env_right.reshape(TERMS * RIGHT_DEV, B, B),
    )


def finish_kernel(first, count, labels, partial, last, out, held, rest, sem, rest_sem):
    parts = held.shape[0] // 8

    def fetch(part):
        rows = pl.ds(part * 8, 8)
        return pltpu.make_async_copy(partial.at[rows], held.at[rows], sem.at[part])

    def store(part):
        rows = pl.ds(part * 8, 8)
        return pltpu.make_async_copy(held.at[rows], out.at[rows], sem.at[part])

    rest_fetch = pltpu.make_async_copy(last, rest, rest_sem)
    rest_fetch.start()
    for part in range(parts):
        fetch(part).start()
    label = label_of(labels, first, count)
    rest_fetch.wait()

    def add(part, carry):
        onehot = onehot_rows(label, part * 256, (256, count * CHIPS))
        fetch(part).wait()
        width = rest.shape[-1]
        for piece in range(rest.shape[0]):
            x, lanes = piece * width // B, piece * width % B
            lanes = slice(lanes, lanes + width)
            total = jnp.dot(
                onehot, rest[piece], preferred_element_type=jnp.float32
            ).reshape(8, SECTORS, width)
            total = total + held[pl.ds(part * 8, 8), x, :, lanes].astype(jnp.float32)
            held[pl.ds(part * 8, 8), x, :, lanes] = total.astype(jnp.bfloat16)
        store(part).start()
        return carry

    lax.fori_loop(0, parts, add, 0)
    for part in range(parts):
        store(part).wait()


def finished(slots, labels, partial, last):
    count = last_count(slots)
    anywhere = pl.BlockSpec(memory_space=pl.ANY)
    return pl.pallas_call(
        functools.partial(finish_kernel, slots - count, count),
        name=f"finish_{slots}",
        out_shape=jax.ShapeDtypeStruct(partial.shape, partial.dtype),
        in_specs=[pl.BlockSpec(memory_space=pltpu.VMEM), anywhere, anywhere],
        out_specs=anywhere,
        scratch_shapes=[
            pltpu.VMEM(partial.shape, partial.dtype),
            pltpu.VMEM(last.shape, last.dtype),
            pltpu.SemaphoreType.DMA((SECTORS // 8,)),
            pltpu.SemaphoreType.DMA,
        ],
        compiler_params=pltpu.CompilerParams(vmem_limit_bytes=VMEM_LIMIT),
        cost_estimate=pl.CostEstimate(
            flops=2 * SECTORS**2 * count * CHIPS * ROWS * B,
            bytes_accessed=9 * 2**20,
            transcendentals=0,
        ),
    )(labels, partial, last)


def local(psi, env_left, env_right, left_target, right_target, qn_left, qn_right):
    items, sources, labels, choice = tables(left_target, right_target, qn_left, qn_right)

    def branch(depth, slots, operands):
        labels = operands[2]
        return finished(slots, labels, *exchanged(depth, slots, *operands))

    return lax.switch(
        choice[0, 0],
        [functools.partial(branch, depth, slots) for depth, slots in SIZES],
        (items, sources, labels, psi, env_left, env_right),
    )


def solution(mesh):
    fine = Mesh(
        mesh.devices.reshape(CHIPS_Z, CORES, RIGHT), ("z", "core", "right")
    )
    left = ("z", "core")
    return jax.shard_map(
        local,
        mesh=fine,
        in_specs=(
            P(left, None, "right", None),
            P(None, left, None, None),
            P(None, "right", None, None),
            P(),
            P(),
            P(),
            P(),
        ),
        out_specs=P(None, ("z", "core", "right"), None, None),
        check_vma=False,
    )
```

```python
import functools

import jax
import jax.numpy as jnp
from jax import lax
from jax.experimental import pallas as pl
from jax.experimental.pallas import tpu as pltpu
from jax.sharding import Mesh, PartitionSpec as P

filling_charge = 3
B = 512
SECTORS = 32
TERMS = 2
CHIPS_Z = 4
CORES = 2
RIGHT = 16
CHIPS = CHIPS_Z * RIGHT
LEFT_DEV = SECTORS // (CHIPS_Z * CORES)
RIGHT_DEV = SECTORS // RIGHT
ITEMS = TERMS * LEFT_DEV * RIGHT_DEV
HALF = B // CORES
ROWS = B // (CHIPS * CORES)
MESH = pl.DeviceIdType.MESH
VMEM_LIMIT = 60 * 2**20
SIZES = ((10, 12), (10, 14), (12, 16), (12, 18), (16, 32))


def table_kernel(left_target, right_target, qn_left, qn_right, items, sources, labels, most):
    f32, bf16 = jnp.float32, jnp.bfloat16
    square = (SECTORS, SECTORS)
    row = lax.broadcasted_iota(jnp.int32, square, 0)
    column = lax.broadcasted_iota(jnp.int32, square, 1)
    wide = lambda value: value.astype(f32)
    dot = lambda a, b: jnp.dot(a.astype(bf16), b.astype(bf16), preferred_element_type=f32)
    upright = lambda line: jnp.sum(
        jnp.where(row == column, wide(line), 0.0), axis=1, keepdims=True
    )
    charge_left = qn_left[...]
    charge_right = upright(qn_right[...])

    pair = wide(row // RIGHT_DEV == column // RIGHT_DEV)
    second = wide((row + 1 == column) & (column % RIGHT_DEV == 1))
    same = row // LEFT_DEV == column // LEFT_DEV
    core = wide(row // LEFT_DEV % CORES)
    swap = wide(column == row + LEFT_DEV - 2 * LEFT_DEV * (row // LEFT_DEV % CORES))
    active, to_left, to_right, rank, total = [], [], [], [], []
    for t in range(TERMS):
        lefts = upright(left_target[t : t + 1, :])
        rights = wide(right_target[t : t + 1, :])
        hit_left = wide(column) == lefts
        hit_right = wide(row) == rights
        have_left = jnp.sum(jnp.where(hit_left, wide(charge_left), 0.0), axis=1, keepdims=True)
        have_right = jnp.sum(jnp.where(hit_right, charge_right, 0.0), axis=0, keepdims=True)
        allowed = have_left + have_right == float(filling_charge)
        ones = jnp.where(allowed, 1.0, 0.0)
        count = dot(ones, pair)
        active.append(allowed)
        to_left.append(lefts)
        to_right.append(rights)
        rank.append(dot(wide(same & (column < row)), count) + dot(ones, second))
        total.append(dot(wide(same), count))
    rank[1] = rank[1] + total[0]
    own = total[0] + total[1]
    other = dot(swap, own)
    slot = [r + jnp.minimum(other, r + core) for r in rank]

    lane = lax.broadcasted_iota(jnp.int32, (SECTORS, 128), 1)
    tall = lax.broadcasted_iota(jnp.int32, (SECTORS, 128), 0)
    device_lane = tall // RIGHT_DEV == lane % RIGHT
    device_row = tall // LEFT_DEV == lane // RIGHT
    chip_row = tall // (CORES * LEFT_DEV) == lane % CHIPS // RIGHT

    def spread(steps, place, values, rows):
        stack = []
        for k in steps:
            picked = jnp.zeros(square, f32)
            for t in range(TERMS):
                picked = picked + jnp.where(
                    active[t] & (place[t] == float(k)), values[t], 0.0
                )
            stack.append(picked.astype(bf16))
        lanes = dot(jnp.concatenate(stack, axis=0), wide(device_lane))
        lanes = lanes.reshape(len(stack), SECTORS, 128)
        return jnp.sum(jnp.where(rows[None], lanes, 0.0), axis=1)

    item = wide(row % LEFT_DEV * RIGHT_DEV + column % RIGHT_DEV)
    items[...] = spread(
        range(ITEMS), rank, [item, item + float(LEFT_DEV * RIGHT_DEV)], device_row
    ).astype(jnp.int32)

    half_lane = lax.broadcasted_iota(jnp.int32, (ITEMS, 128), 1)

    def by_slot(values):
        both = spread(
            [*range(0, 2 * ITEMS, 2), *range(1, 2 * ITEMS, 2)], slot, values, chip_row
        )
        return jnp.where(half_lane < CHIPS, both[:ITEMS], both[ITEMS:])

    sources[...] = by_slot([core * ITEMS + r for r in rank]).astype(jnp.int32)
    full = jnp.zeros(square, f32)
    high = by_slot([full + lefts + 1.0 for lefts in to_left])
    low = by_slot([full + rights for rights in to_right])
    labels[...] = ((high - 1.0) * SECTORS + low).astype(jnp.int32)
    most_device = jnp.max(own)
    most_chip = jnp.max(own + other)
    choice = jnp.int32(0)
    for depth, slots in SIZES[:-1]:
        choice = choice + jnp.where(
            (most_device > float(depth)) | (most_chip > float(slots)), 1, 0
        )
    most[0, 0] = choice


def tables(left_target, right_target, qn_left, qn_right):
    vmem = pl.BlockSpec(memory_space=pltpu.VMEM)
    table = jax.ShapeDtypeStruct((ITEMS, 128), jnp.int32)
    return pl.pallas_call(
        table_kernel,
        name="tables",
        out_shape=[table, table, table, jax.ShapeDtypeStruct((1, 1), jnp.int32)],
        in_specs=[vmem] * 4,
        out_specs=[vmem] * 3 + [pl.BlockSpec(memory_space=pltpu.SMEM)],
        cost_estimate=pl.CostEstimate(flops=2**24, bytes_accessed=2**15, transcendentals=0),
    )(
        left_target,
        right_target,
        qn_left.reshape(1, SECTORS),
        qn_right.reshape(1, SECTORS),
    )


def fours_of(slots):
    return (slots - 2) // 4


def last_count(slots):
    return 4 if slots % 4 == 2 else 2


def last_shape(count):
    return ROWS * 4 // count, count * CHIPS, B * count // 4


def onehot_rows(label, first, shape):
    row = first + lax.broadcasted_iota(jnp.int32, shape, 0)
    return jnp.where(row == label, 1.0, 0.0).astype(jnp.bfloat16)


def label_of(labels, first, count):
    return jnp.concatenate(
        [labels[pl.ds(first // 2 + p, 1), :] for p in range(count // 2)], axis=1
    )


def exchange(shape_from, shape_to):
    row = lax.broadcasted_iota(jnp.int32, (256, 256), 0)
    column = lax.broadcasted_iota(jnp.int32, (256, 256), 1)
    source = row % shape_from * shape_to + row // shape_from
    return jnp.where(column == source, 1.0, 0.0).astype(jnp.bfloat16)


def reorder(onehot, rows):
    return jnp.dot(onehot, rows, preferred_element_type=jnp.float32).astype(jnp.bfloat16)


def order(incoming, count, sorted_rows):
    unsort = exchange(16, 16)

    def sort(far_z, carry):
        rows = incoming[pl.ds(far_z * RIGHT, RIGHT)]
        rows = reorder(unsort, rows.reshape(256, rows.shape[-1]))
        for piece in range(16):
            start = pl.multiple_of(piece % count * CHIPS + far_z * RIGHT, RIGHT)
            sorted_rows[piece // count, pl.ds(start, RIGHT), :] = rows[
                piece * RIGHT : (piece + 1) * RIGHT
            ]
        return carry

    lax.fori_loop(0, CHIPS_Z, sort, 0, unroll=2)


def exchange_kernel(
    depth,
    slots,
    items,
    sources,
    labels,
    psi_hbm,
    left_hbm,
    right_hbm,
    out,
    last,
    landed,
    psi,
    left,
    right,
    product,
    both,
    send,
    arrived,
    send_pair,
    arrived_pair,
    partial,
    ordered,
    ordered_pair,
    in_sem,
    own_sem,
    pair_send_sem,
    pair_recv_sem,
    free_sem,
    self_sem,
    send_sem,
    recv_sem,
    out_sem,
):
    z = lax.axis_index("z")
    core = lax.axis_index("core")
    place = lax.axis_index("right")
    other = 1 - core
    partner = (z, other, place)
    here = z * RIGHT + place
    device = (z * CORES + core) * RIGHT + place
    fours = fours_of(slots)
    stages = -(-(depth + 2) // 4)
    ends_in_pair = last_count(slots) == 2

    psi_rows = psi_hbm.reshape(LEFT_DEV, B * RIGHT_DEV, B)
    psi_load = [
        pltpu.make_async_copy(psi_rows.at[a], landed.at[a], in_sem.at[a])
        for a in range(LEFT_DEV)
    ]
    left_load = pltpu.make_async_copy(left_hbm, left, in_sem.at[LEFT_DEV])
    right_load = pltpu.make_async_copy(right_hbm, right, in_sem.at[LEFT_DEV + 1])
    for load in (*psi_load, left_load, right_load):
        load.start()

    steps = (1, 3, 2, 0)
    way = 1 - 2 * core
    route = []
    for i in range(RIGHT):
        step_x = steps[i % 4]
        step_y = steps[(i + i // 4) % 4]
        far_x = (place // 4 + 4 + way * step_x) % 4
        far_y = (place % 4 + 4 + way * step_y) % 4
        route.append((step_x + step_y, steps[(i + i // 4 * 2) % 4], far_x * 4 + far_y))

    def for_others(visit):
        def turn(shift, carry):
            far_z = [
                (z + 2 * CHIPS_Z + way * (shift + step)) % CHIPS_Z for step in range(CHIPS_Z)
            ]
            for moved, step, far_place in route:
                if moved or step:
                    visit(far_z[step], far_place)
                else:
                    pl.when(shift > 0)(functools.partial(visit, far_z[step], far_place))
            return carry

        lax.fori_loop(0, CHIPS_Z, turn, 0)

    barrier = pltpu.get_barrier_semaphore()
    pl.semaphore_signal(barrier, inc=1, device_id=partner, device_id_type=MESH)

    def greet(far_z, far_place):
        pl.semaphore_signal(
            barrier, inc=1, device_id=(far_z, core, far_place), device_id_type=MESH
        )

    def greet_turn(shift):
        far_z = [
            (z + 2 * CHIPS_Z + way * (shift + step)) % CHIPS_Z for step in range(CHIPS_Z)
        ]
        for moved, step, far_place in route:
            if moved or step:
                greet(far_z[step], far_place)

    for step in range(1, CHIPS_Z):
        greet((z + step) % CHIPS_Z, place)
    greet_turn(0)

    unmix = exchange(128, RIGHT_DEV)

    def split(a):
        for part in range(B // 128):
            apart = reorder(unmix, landed[a, part * 256 : part * 256 + 256, :])
            for b in range(RIGHT_DEV):
                psi[a * RIGHT_DEV + b, part * 128 : part * 128 + 128, :] = apart[
                    b * 128 : (b + 1) * 128
                ]

    def greet_and_split(a, carry):
        pltpu.make_async_copy(psi_rows.at[a], landed.at[a], in_sem.at[a]).wait()
        greet_turn(a + 1)
        split(a)
        return carry

    lax.fori_loop(0, LEFT_DEV - 1, greet_and_split, 0)
    psi_load[LEFT_DEV - 1].wait()
    split(LEFT_DEV - 1)
    left_load.wait()
    right_load.wait()

    def own_copy(rank):
        return pltpu.make_async_copy(
            product.at[rank, :, core], both.at[core * depth + rank], own_sem.at[rank]
        )

    def pair_copy(rank):
        return pltpu.make_async_remote_copy(
            src_ref=product.at[rank, :, other],
            dst_ref=both.at[core * depth + rank],
            send_sem=pair_send_sem.at[rank],
            recv_sem=pair_recv_sem.at[rank],
            device_id=partner,
            device_id_type=MESH,
        )

    def multiply_two(step):
        ranks = (2 * step, 2 * step + 1)
        halves, rights = [], []
        for rank in ranks:
            item = items[rank, device]
            term = item // (LEFT_DEV * RIGHT_DEV)
            pair = item % (LEFT_DEV * RIGHT_DEV)
            half = jnp.dot(
                left[term * LEFT_DEV + pair // RIGHT_DEV],
                psi[pair],
                preferred_element_type=jnp.float32,
            )
            halves.append(half.astype(jnp.bfloat16))
            rights.append(right[term * RIGHT_DEV + pair % RIGHT_DEV])
        for rank, half, by in zip(ranks, halves, rights):
            moved = lax.dot_general(
                half, by, (((1,), (1,)), ((), ())), preferred_element_type=jnp.float32
            ).astype(jnp.bfloat16)
            product[rank] = moved.reshape(CHIPS_Z, CORES, B // (CHIPS_Z * CORES), B)

    def swap_two(step):
        @pl.when(step == 0)
        def _():
            pl.semaphore_wait(barrier, CHIPS)

        @pl.when((step > 0) & (step % 2 == 1))
        def _():
            pl.semaphore_wait(free_sem, 1)

        for rank in (2 * step, 2 * step + 1):
            pair_copy(rank).start()
            own_copy(rank).start()

    def advance(step, carry):
        pl.when(step >= 0)(lambda: swap_two(step))
        pl.when(step + 1 < depth // 2)(lambda: multiply_two(step + 1))
        return carry

    def arrive(rank, carry):
        own_copy(rank).wait()
        pair_copy(rank).wait_recv()
        return carry

    def departing(outgoing, incoming, chunk, far_z, far_place):
        pltpu.make_async_remote_copy(
            src_ref=outgoing.at[far_z * RIGHT + far_place],
            dst_ref=incoming.at[here],
            send_sem=send_sem.at[chunk],
            recv_sem=recv_sem.at[chunk],
            device_id=(far_z, core, far_place),
            device_id_type=MESH,
        ).start()

    def self_copy(outgoing, incoming, chunk):
        return pltpu.make_async_copy(
            outgoing.at[here], incoming.at[here], self_sem.at[chunk]
        )

    mix = exchange(4, 64)

    def pack(outgoing, first, count):
        def quarter(far_z, carry):
            def block(k):
                source = sources[first // 2 + k // 2, k % 2 * CHIPS + here]
                return both[source // ITEMS * depth + source % ITEMS, far_z]

            blocks = [block(k) for k in range(count)]
            if count == 2:
                blocks = [rows[:, : B // 2] for rows in blocks] + [rows[:, B // 2 :] for rows in blocks]
            rows = reorder(mix, jnp.concatenate(blocks, axis=0))
            outgoing[pl.ds(far_z * RIGHT, RIGHT)] = rows.reshape(
                RIGHT, 4 * ROWS, rows.shape[-1]
            )
            return carry

        lax.fori_loop(0, CHIPS_Z, quarter, 0, unroll=2)

    def depart(outgoing, incoming, chunk):
        self_copy(outgoing, incoming, chunk).start()
        for_others(functools.partial(departing, outgoing, incoming, chunk))

    def stage(turn, carry):
        start = jnp.maximum(4 * turn - 2, 0)
        stop = jnp.maximum(jnp.minimum(4 * turn + 2, depth), start)
        lax.fori_loop(jnp.where(turn == 0, -1, start // 2), stop // 2, advance, 0)
        lax.fori_loop(start, stop, arrive, 0)

        four = jnp.maximum(turn - 1, 0)
        pl.when(turn == 0)(lambda: pack(send_pair.at[0], 0, 2))
        pl.when(turn > 0)(lambda: pack(send.at[four], 2 + 4 * four, 4))

        @pl.when(turn < stages - 1)
        def _():
            pl.semaphore_signal(free_sem, inc=1, device_id=partner, device_id_type=MESH)

        pl.when(turn == 0)(lambda: depart(send_pair.at[0], arrived_pair.at[0], fours))
        pl.when(turn > 0)(lambda: depart(send.at[four], arrived.at[four], four))
        return carry

    lax.fori_loop(0, fours + 1, stage, 0)
    if ends_in_pair:
        pack(send_pair.at[1], slots - 2, 2)
        depart(send_pair.at[1], arrived_pair.at[1], fours + 1)

    def receive(outgoing, incoming, chunk):
        self_copy(outgoing, incoming, chunk).wait()
        arrivals = incoming.at[pl.ds(0, CHIPS - 1)]
        pltpu.make_async_copy(arrivals, arrivals, recv_sem.at[chunk]).wait()

    partial[...] = jnp.zeros(partial.shape, partial.dtype)

    def place_chunk(first, count, sorted_rows):
        label = label_of(labels, first, count)
        pieces, _, width = sorted_rows.shape

        def put(part, carry):
            onehot = onehot_rows(label, part * 256, (256, count * CHIPS))

            def row(x, carry):
                for half in range(pieces // ROWS):
                    lanes = slice(half * width, half * width + width)
                    total = jnp.dot(
                        onehot,
                        sorted_rows[x * (pieces // ROWS) + half],
                        preferred_element_type=jnp.float32,
                    ).reshape(8, SECTORS, width)
                    total = total + partial[pl.ds(part * 8, 8), x, :, lanes].astype(jnp.float32)
                    partial[pl.ds(part * 8, 8), x, :, lanes] = total.astype(jnp.bfloat16)
                return carry

            return lax.fori_loop(0, ROWS, row, carry, unroll=2)

        lax.fori_loop(0, SECTORS // 8, put, 0)

    receive(send_pair.at[0], arrived_pair.at[0], fours)
    order(arrived_pair.at[0], 2, ordered_pair)
    place_chunk(0, 2, ordered_pair)
    placed = fours if ends_in_pair else fours - 1

    def collect(four, carry):
        receive(send.at[four], arrived.at[four], four)
        order(arrived.at[four], 4, ordered)

        @pl.when(four < placed)
        def _():
            place_chunk(2 + 4 * four, 4, ordered)

        @pl.when(four == placed - 1)
        def _():
            pltpu.make_async_copy(partial, out, out_sem.at[0]).start()

        return carry

    lax.fori_loop(0, fours, collect, 0)
    rest = ordered
    if ends_in_pair:
        receive(send_pair.at[1], arrived_pair.at[1], fours + 1)
        order(arrived_pair.at[1], 2, ordered_pair)
        rest = ordered_pair
    rest_out = pltpu.make_async_copy(rest, last, out_sem.at[1])
    rest_out.start()

    def sent(rank, carry):
        pair_copy(rank).wait_send()
        return carry

    lax.fori_loop(0, depth, sent, 0)

    def gone(chunk, carry):
        departures = send.at[chunk, pl.ds(0, CHIPS - 1)]
        pltpu.make_async_copy(departures, departures, send_sem.at[chunk]).wait()
        return carry

    lax.fori_loop(0, fours, gone, 0)
    for pair in range(1 + ends_in_pair):
        departures = send_pair.at[pair, pl.ds(0, CHIPS - 1)]
        pltpu.make_async_copy(departures, departures, send_sem.at[fours + pair]).wait()
    pltpu.make_async_copy(partial, out, out_sem.at[0]).wait()
    rest_out.wait()


def exchanged(depth, slots, items, sources, labels, psi, env_left, env_right):
    smem = pl.BlockSpec(memory_space=pltpu.SMEM)
    anywhere = pl.BlockSpec(memory_space=pl.ANY)
    vmem = pl.BlockSpec(memory_space=pltpu.VMEM)
    bf16 = jnp.bfloat16
    fours = fours_of(slots)
    messages = (CHIPS, 4 * ROWS, B)
    pair_messages = (2, CHIPS, 4 * ROWS, B // 2)
    dma = pltpu.SemaphoreType.DMA
    return pl.pallas_call(
        functools.partial(exchange_kernel, depth, slots),
        name=f"exchange_{slots}",
        out_shape=[
            jax.ShapeDtypeStruct((SECTORS, ROWS, SECTORS, B), bf16),
            jax.ShapeDtypeStruct(last_shape(last_count(slots)), bf16),
        ],
        in_specs=[smem] * 2 + [vmem] + [anywhere] * 3,
        out_specs=[anywhere] * 2,
        scratch_shapes=[
            pltpu.VMEM((LEFT_DEV, B * RIGHT_DEV, B), bf16),
            pltpu.VMEM((LEFT_DEV * RIGHT_DEV, B, B), bf16),
            pltpu.VMEM((TERMS * LEFT_DEV, B, B), bf16),
            pltpu.VMEM((TERMS * RIGHT_DEV, B, B), bf16),
            pltpu.VMEM((depth, CHIPS_Z, CORES, B // (CHIPS_Z * CORES), B), bf16),
            pltpu.VMEM((CORES * depth, CHIPS_Z, B // (CHIPS_Z * CORES), B), bf16),
            pltpu.VMEM((fours, *messages), bf16),
            pltpu.VMEM((fours, *messages), bf16),
            pltpu.VMEM(pair_messages, bf16),
            pltpu.VMEM(pair_messages, bf16),
            pltpu.VMEM((SECTORS, ROWS, SECTORS, B), bf16),
            pltpu.VMEM(last_shape(4), bf16),
            pltpu.VMEM(last_shape(2), bf16),
            dma((LEFT_DEV + 2,)),
            dma((depth,)),
            dma((depth,)),
            dma((depth,)),
            pltpu.SemaphoreType.REGULAR,
            dma((fours + 2,)),
            dma((fours + 2,)),
            dma((fours + 2,)),
            dma((2,)),
        ],
        compiler_params=pltpu.CompilerParams(
            collective_id=slots // 2,
            has_side_effects=True,
            vmem_limit_bytes=VMEM_LIMIT,
        ),
        cost_estimate=pl.CostEstimate(
            flops=4 * depth * B**3, bytes_accessed=14 * 2**20, transcendentals=0
        ),
    )(
        items,
        sources,
        labels,
        psi,
        env_left.reshape(TERMS * LEFT_DEV, B, B),
        env_right.reshape(TERMS * RIGHT_DEV, B, B),
    )


def finish_kernel(first, count, labels, partial, last, out, held, rest, sem, rest_sem):
    parts = held.shape[0] // 8

    def fetch(part):
        rows = pl.ds(part * 8, 8)
        return pltpu.make_async_copy(partial.at[rows], held.at[rows], sem.at[part])

    def store(part):
        rows = pl.ds(part * 8, 8)
        return pltpu.make_async_copy(held.at[rows], out.at[rows], sem.at[part])

    rest_fetch = pltpu.make_async_copy(last, rest, rest_sem)
    rest_fetch.start()
    for part in range(parts):
        fetch(part).start()
    label = label_of(labels, first, count)
    rest_fetch.wait()

    def add(part, carry):
        onehot = onehot_rows(label, part * 256, (256, count * CHIPS))
        fetch(part).wait()
        width = rest.shape[-1]
        for piece in range(rest.shape[0]):
            x, lanes = piece * width // B, piece * width % B
            lanes = slice(lanes, lanes + width)
            total = jnp.dot(
                onehot, rest[piece], preferred_element_type=jnp.float32
            ).reshape(8, SECTORS, width)
            total = total + held[pl.ds(part * 8, 8), x, :, lanes].astype(jnp.float32)
            held[pl.ds(part * 8, 8), x, :, lanes] = total.astype(jnp.bfloat16)
        store(part).start()
        return carry

    lax.fori_loop(0, parts, add, 0)
    for part in range(parts):
        store(part).wait()


def finished(slots, labels, partial, last):
    count = last_count(slots)
    anywhere = pl.BlockSpec(memory_space=pl.ANY)
    return pl.pallas_call(
        functools.partial(finish_kernel, slots - count, count),
        name=f"finish_{slots}",
        out_shape=jax.ShapeDtypeStruct(partial.shape, partial.dtype),
        in_specs=[pl.BlockSpec(memory_space=pltpu.VMEM), anywhere, anywhere],
        out_specs=anywhere,
        scratch_shapes=[
            pltpu.VMEM(partial.shape, partial.dtype),
            pltpu.VMEM(last.shape, last.dtype),
            pltpu.SemaphoreType.DMA((SECTORS // 8,)),
            pltpu.SemaphoreType.DMA,
        ],
        compiler_params=pltpu.CompilerParams(vmem_limit_bytes=VMEM_LIMIT),
        cost_estimate=pl.CostEstimate(
            flops=2 * SECTORS**2 * count * CHIPS * ROWS * B,
            bytes_accessed=9 * 2**20,
            transcendentals=0,
        ),
    )(labels, partial, last)


def local(psi, env_left, env_right, left_target, right_target, qn_left, qn_right):
    items, sources, labels, choice = tables(left_target, right_target, qn_left, qn_right)

    def branch(depth, slots, operands):
        labels = operands[2]
        return finished(slots, labels, *exchanged(depth, slots, *operands))

    return lax.switch(
        choice[0, 0],
        [functools.partial(branch, depth, slots) for depth, slots in SIZES],
        (items, sources, labels, psi, env_left, env_right),
    )


def solution(mesh):
    fine = Mesh(
        mesh.devices.reshape(CHIPS_Z, CORES, RIGHT), ("z", "core", "right")
    )
    left = ("z", "core")
    return jax.shard_map(
        local,
        mesh=fine,
        in_specs=(
            P(left, None, "right", None),
            P(None, left, None, None),
            P(None, "right", None, None),
            P(),
            P(),
            P(),
            P(),
        ),
        out_specs=P(None, ("z", "core", "right"), None, None),
        check_vma=False,
    )
```
